32 devices in a mesh: doc: 8 (over y, x, core), lab: 4 (over z).
Axes of the slice: x: 2, y: 2, z: 4, core: 2. Of those that a mesh axis runs over, the one named last changes fastest.
Arguments:
- embeddings: bfloat16 [16384, 768], P(('doc', 'lab')), may hold values from -6 to 6
- positives: int32 [16384, 16], P(('doc', 'lab')), may hold values from 0 to 4095, as said below
- weights: float32 [8192, 768], P(('doc', 'lab')), may hold values from -6 to 6
- parents: int32 [8192], replicated, may hold values from 0 to 254, as said below
- owners: int32 [4, 8], replicated, may hold values from 0 to 3
- shortlist: int32 [4, 32, 4], replicated, may hold values from 0 to 3, as said below
- counts: int32 [4, 32], replicated, may hold values from 1 to 4, as said below
Outputs:
- trained: float32 [8192, 768], P(('doc', 'lab'))
- momentum: float32 [8192, 768], P(('doc', 'lab'))
The draws below stay inside these ranges and needn't reach their ends.
Inputs may be any that keep to these rules, and one draw needn't show every extreme that they name: `positives`: each positive code is (s * 4 + j) * 256 + l with s < 4, j < 4, l < 256; repeats allowed. parents[l] is a row of l's own block below l's row; row 0 of a block is its own parent. `shortlist`: the 4 tile numbers of one step and block are distinct. `counts`: in every step some block has all 4 slots live.
All inputs are finite; a program needn't handle non-finite values.
Results may differ from the reference program's by a relative error of at most 0.0003.
Values may be sent and summed in bfloat16 or wider, within the bound.
No kernel may reach another device: no remote copies, remote signals or barrier semaphores. Data moves between devices by JAX's collectives and lax.ppermute only.
A program may use at most 64 MiB of HBM per device.

```python
import jax
import jax.numpy as jnp
from jax import lax

D = 768
BLOCK = 256
TILE = 128
PANEL = 512
MAXT = 4
POS = 16
STEPS = 4
DGROUPS = 8
LGROUPS = 4
TILES = 4
LBLOCKS = 32
LABELS = 8192
DOCS = 16384
N_LAB = 4


def draw_positives(key, part):
    rows = DGROUPS * LGROUPS * PANEL
    key_step, key_lab, key_off = jax.random.split(jax.random.fold_in(key, 11), 3)
    step = jax.random.randint(key_step, (rows, POS), 0, STEPS)
    label_group = jax.random.randint(key_lab, (rows, POS), 0, LGROUPS)
    offset = jax.random.randint(key_off, (rows, POS), 0, BLOCK)
    result = ((step * LGROUPS + label_group) * BLOCK + offset).astype(jnp.int32)
    result = result.at[0, 0].set(0)
    result = result.at[rows - 1, POS - 1].set(STEPS * LGROUPS * BLOCK - 1)
    return result


def draw_parents(key, part):
    local = jnp.arange(LABELS, dtype=jnp.int32) % BLOCK
    picked = jax.random.randint(jax.random.fold_in(key, 12), (LABELS,), 0, jnp.maximum(local, 1))
    picked = jnp.where(local == 0, 0, picked)
    picked = jnp.where(local == BLOCK - 1, BLOCK - 2, picked)
    return picked.astype(jnp.int32)


def draw_shortlist(key, part):
    keys = jax.random.split(jax.random.fold_in(key, 13), STEPS * LBLOCKS)
    picks = jax.vmap(lambda one_key: jax.random.permutation(one_key, TILES)[:MAXT])(keys)
    return picks.reshape(STEPS, LBLOCKS, MAXT).astype(jnp.int32)


def draw_counts(key, part):
    key_level, key_full = jax.random.split(jax.random.fold_in(key, 14))
    result = jax.random.randint(key_level, (STEPS, LBLOCKS), 1, MAXT + 1)
    full_block = jax.random.randint(key_full, (STEPS,), 0, LBLOCKS)
    result = result.at[jnp.arange(STEPS), full_block].set(MAXT)
    return result.astype(jnp.int32)


def plant(drawn, rng, least, largest):
    extent = drawn.shape
    place = [jax.random.randint(jax.random.fold_in(rng, axis), (), 0, extent[axis]) for axis in range(len(extent))]
    drawn = drawn.at[tuple(place)].set(least)
    longest = extent.index(max(extent))
    place[longest] = (place[longest] + 1) % extent[longest]
    return drawn.at[tuple(place)].set(largest)


def shard_levels(own_key, shape, cuts, smallest, largest):
    level = 1.0
    for position, blocks in cuts:
        steps = jax.random.uniform(jax.random.fold_in(jax.random.fold_in(own_key, 6), position), (blocks,), jnp.float32, smallest / len(cuts), largest / len(cuts))
        level = level * jnp.repeat(jnp.exp(steps), shape[position] // blocks).reshape((-1,) + (1,) * (len(shape) - 1 - position))
    return level


def gaussian(own_key, shape, spread, bound, cuts=(), kind=jnp.bfloat16):
    array = jax.random.normal(own_key, shape, jnp.float32) * spread
    if len(cuts) > 0:
        array = shard_levels(own_key, shape, cuts, -0.22, 0.18) * array
    return jnp.clip(array, min=-bound, max=bound).astype(kind)


def setup_inputs(seed: int = 0) -> dict:
    seeds = jax.random.split(jax.random.key(seed), 8)
    embeddings = gaussian(seeds[0], (DOCS, D), 1.0, 6.0, ((0, 32),))
    positives = draw_positives(jax.random.fold_in(seeds[7], 71), 0)
    weights = gaussian(seeds[2], (LABELS, D), 1.0, 6.0, ((0, 32),), jnp.float32)
    parents = draw_parents(jax.random.fold_in(seeds[7], 71), 0)
    owners = plant(jax.random.randint(seeds[4], (STEPS, DGROUPS), 0, N_LAB), jax.random.fold_in(seeds[4], 1), 0, N_LAB - 1).astype(jnp.int32)
    shortlist = draw_shortlist(jax.random.fold_in(seeds[7], 71), 0)
    counts = draw_counts(jax.random.fold_in(seeds[7], 71), 0)
    return {"embeddings": embeddings, "positives": positives, "weights": weights, "parents": parents, "owners": owners, "shortlist": shortlist, "counts": counts}


learning_rate = 0.1
beta_rate = 0.9
pull_rate = 1.0

def pick_rows(panel, labels, tiles, tile_rows):
    width = panel.shape[1]
    shaped = panel.reshape(panel.shape[0] // tile_rows, tile_rows, width)
    lshaped = labels.reshape(labels.shape[0] // tile_rows, tile_rows, labels.shape[1])
    rows = jnp.take(shaped, tiles, axis=0).reshape(tiles.shape[0] * tile_rows, width)
    picked = jnp.take(lshaped, tiles, axis=0).reshape(tiles.shape[0] * tile_rows, labels.shape[1])
    return (rows, picked)

def block_update(weight, moment, rows, picked, base, parent_rows, live):
    scale = 1.0 / jnp.sqrt(jnp.float32(rows.shape[1]))
    rows32 = rows.astype(jnp.float32)
    scores = jnp.dot(rows32, weight.T, precision=lax.Precision.HIGHEST, preferred_element_type=jnp.float32) * scale
    label_ids = base + jnp.arange(weight.shape[0], dtype=jnp.int32)
    target = jnp.any(picked[:, :, None] == label_ids[None, None, :], axis=1).astype(jnp.float32)
    resid = (jax.nn.sigmoid(scores) - target) * live[:, None]
    grad = jnp.dot(resid.T, rows32, precision=lax.Precision.HIGHEST, preferred_element_type=jnp.float32) * scale
    grad = grad + pull_rate * (weight - jnp.take(weight, parent_rows, axis=0))
    moment = beta_rate * moment + grad
    return (weight - learning_rate * moment, moment)

def reference(embeddings, positives, weights, parents, owners, shortlist, counts):
    blocks = weights.reshape(LBLOCKS, BLOCK, D)
    moments = jnp.zeros((LBLOCKS, BLOCK, D), jnp.float32)
    parent_blocks = parents.reshape(LBLOCKS, BLOCK)
    slot_of_row = jnp.arange(MAXT * TILE, dtype=jnp.int32) // TILE
    for step in range(STEPS):

        def one(item):
            index, weight, moment, parent_rows = item
            anchor = index // LGROUPS
            holder = (anchor + step) % DGROUPS
            owner = owners[step, holder]
            start = ((holder * LGROUPS + owner) * PANEL).astype(jnp.int32)
            panel = lax.dynamic_slice_in_dim(embeddings, start, PANEL, 0)
            labels = lax.dynamic_slice_in_dim(positives, start, PANEL, 0)
            rows, picked = pick_rows(panel, labels, shortlist[step, index], TILE)
            live = (slot_of_row < counts[step, index]).astype(jnp.float32)
            base = ((step * LGROUPS + index % LGROUPS) * BLOCK).astype(jnp.int32)
            return block_update(weight, moment, rows, picked, base, parent_rows, live)
        blocks, moments = lax.map(one, (jnp.arange(LBLOCKS, dtype=jnp.int32), blocks, moments, parent_blocks))
    return (blocks.reshape(LABELS, D), moments.reshape(LABELS, D))
```

```python
import functools

import jax
import jax.numpy as jnp
from jax import lax
from jax.experimental import pallas as pl
from jax.experimental.pallas import tpu as pltpu
from jax.sharding import PartitionSpec as P

TILE = 128
STEPS = 4
CHUNKS = 2
CODE_ROWS = 16

learning_rate = 0.1
beta_rate = 0.9
pull_rate = 1.0

VMEM = pl.BlockSpec(memory_space=pltpu.VMEM)
SMEM = pl.BlockSpec(memory_space=pltpu.SMEM)
ANY = pl.BlockSpec(memory_space=pl.ANY)


def select_kernel(n, which_ref, *refs):
    sources, outs, sem = refs[:n], refs[n:-1], refs[-1]
    for k, out in enumerate(outs):
        for i, source in enumerate(sources):

            @pl.when(which_ref[k] == i)
            def _(source=source, out=out, k=k):
                pltpu.make_async_copy(source, out, sem.at[k]).start()

    for k, out in enumerate(outs):
        pltpu.make_async_copy(sources[0], out, sem.at[k]).wait()


def select(which, sources, count):
    shape = jax.ShapeDtypeStruct(sources[0].shape, sources[0].dtype)
    size = sources[0].size * sources[0].dtype.itemsize
    return pl.pallas_call(
        functools.partial(select_kernel, len(sources)),
        out_shape=[shape] * count,
        in_specs=[SMEM] + [ANY] * len(sources),
        out_specs=[ANY] * count,
        scratch_shapes=[pltpu.SemaphoreType.DMA((count,))],
        cost_estimate=pl.CostEstimate(flops=0, bytes_accessed=2 * count * size, transcendentals=0),
        name="select_panels",
    )(which, *sources)


def split(value):
    high = value.astype(jnp.bfloat16)
    return high, (value - high.astype(jnp.float32)).astype(jnp.bfloat16)


def product(pair, other, dims):
    dot = functools.partial(
        lax.dot_general, dimension_numbers=(dims, ((), ())), preferred_element_type=jnp.float32
    )
    return dot(pair[1], other) + dot(pair[0], other)


def update_kernel(first, rows, scale, flags_ref, *refs):
    panels, refs = refs[:CHUNKS], refs[CHUNKS:]
    if first:
        parents_ref, weight_ref, weight_out, moment_out = refs
    else:
        parents_ref, weight_ref, moment_ref, weight_out, moment_out = refs
    labels = weight_ref.shape[0]
    weight = weight_ref[...]
    pair = split(weight)
    label = lax.broadcasted_iota(jnp.int32, (labels, rows), 0).astype(jnp.float32)
    group = flags_ref[0].astype(jnp.float32)
    grad = jnp.zeros(weight.shape, jnp.float32)
    for c, panel_ref in enumerate(panels):
        panel = panel_ref[:rows, :]
        codes = panel_ref[rows:, :].astype(jnp.float32)
        own = jnp.where(codes[:, rows : 2 * rows] == group, codes[:, :rows], -1.0)
        hit = label == own[0:1, :]
        for k in range(1, CODE_ROWS):
            hit = hit | (label == own[k : k + 1, :])
        scores = product(pair, panel, ((1,), (1,))) * scale
        resid = jax.nn.sigmoid(scores) - jnp.where(hit, 1.0, 0.0)
        parts = []
        for t in range(rows // TILE):
            live = flags_ref[1 + c * (rows // TILE) + t].astype(jnp.float32)
            parts.append(resid[:, t * TILE : (t + 1) * TILE] * live)
        resid = jnp.concatenate(parts, axis=1)
        grad = grad + product(split(resid), panel, ((1,), (0,)))
    column = lax.broadcasted_iota(jnp.int32, (labels, labels), 1)
    pick = (column == parents_ref[...]).astype(jnp.bfloat16)
    rest = (weight - pair[0].astype(jnp.float32) - pair[1].astype(jnp.float32)).astype(jnp.bfloat16)
    dot = functools.partial(jnp.dot, preferred_element_type=jnp.float32)
    parent = dot(pick, rest) + dot(pick, pair[1]) + dot(pick, pair[0])
    grad = grad * scale + pull_rate * (weight - parent)
    moment = grad if first else beta_rate * moment_ref[...] + grad
    moment_out[...] = moment
    weight_out[...] = weight - learning_rate * moment


def update(flags, panels, rows, parents, weight, moment):
    labels, width = weight.shape
    first = moment is None
    state = [weight] if first else [weight, moment]
    shape = jax.ShapeDtypeStruct(weight.shape, jnp.float32)
    flops = 8 * labels * width * rows * CHUNKS
    size = 2 * rows * CHUNKS * width + 16 * labels * width
    return pl.pallas_call(
        functools.partial(update_kernel, first, rows, 1.0 / float(width) ** 0.5),
        out_shape=[shape, shape],
        in_specs=[SMEM] + [VMEM] * (len(panels) + 1 + len(state)),
        out_specs=[VMEM, VMEM],
        compiler_params=pltpu.CompilerParams(vmem_limit_bytes=32 * 1024 * 1024),
        cost_estimate=pl.CostEstimate(
            flops=flops, bytes_accessed=size, transcendentals=labels * rows * CHUNKS
        ),
        name="update_block",
    )(flags, *panels, parents, *state)


def gather_line(value, axis):
    n = lax.axis_size(axis)
    up, down = [value], [value]
    for r in range(1, n):
        up.append(lax.ppermute(up[-1], axis, [(i, i + 1) for i in range(r - 1, n - 1)]))
        down.append(lax.ppermute(down[-1], axis, [(i, i - 1) for i in range(1, n - r + 1)]))
    return up[:0:-1] + down


def local(embeddings, positives, weights, parents, owners, shortlist, counts):
    doc_index = lax.axis_index("doc")
    lab_index = lax.axis_index("lab")
    doc_count = lax.axis_size("doc")
    lab_count = lax.axis_size("lab")
    labels, width = weights.shape
    rows = embeddings.shape[0] // CHUNKS
    tiles = embeddings.shape[0] // TILE
    home = doc_index * lab_count + lab_index

    groups = positives // labels
    within = positives - groups * labels
    chunks = []
    for c in range(CHUNKS):
        part = slice(c * rows, (c + 1) * rows)
        codes = jnp.concatenate([within[part].T, groups[part].T], axis=1).astype(jnp.bfloat16)
        codes = jnp.pad(codes, ((0, 0), (0, width - 2 * rows)))
        chunks.append(jnp.concatenate([embeddings[part], codes], axis=0))

    which = lax.dynamic_index_in_dim(owners, doc_index, 1, keepdims=False) - lab_index + lab_count - 1
    lists = lax.dynamic_index_in_dim(shortlist, home, 1, keepdims=False)
    live = lax.dynamic_index_in_dim(counts, home, 1, keepdims=True)
    listed = lists[:, :, None] == jnp.arange(tiles, dtype=jnp.int32)
    used = jnp.arange(lists.shape[1], dtype=jnp.int32) < live
    on = jnp.any(listed & used[:, :, None], axis=1).astype(jnp.int32)
    group = jnp.arange(STEPS, dtype=jnp.int32)[:, None] * lab_count + lab_index
    flags = jnp.concatenate([group, on], axis=1)
    parent_rows = lax.dynamic_slice_in_dim(parents, home * labels, labels, 0)[:, None]

    panels = [[] for _ in range(STEPS)]
    for chunk in chunks:
        found = select(which, gather_line(chunk, "lab"), STEPS)
        for step in range(STEPS):
            got = found[step]
            if step > 0:
                pairs = [(i, (i - step) % doc_count) for i in range(doc_count)]
                got = lax.ppermute(got, "doc", pairs)
            panels[step].append(got)
    weight, moment = weights, None
    for step in range(STEPS):
        weight, moment = update(flags[step], panels[step], rows, parent_rows, weight, moment)
    return (weight, moment)


def solution(mesh):
    return jax.shard_map(
        local,
        mesh=mesh,
        in_specs=(
            P(("doc", "lab"), None),
            P(("doc", "lab"), None),
            P(("doc", "lab"), None),
            P(),
            P(),
            P(),
            P(),
        ),
        out_specs=(P(("doc", "lab"), None), P(("doc", "lab"), None)),
        check_vma=False,
    )
```

```python
import functools

import jax
import jax.numpy as jnp
from jax import lax
from jax.experimental import pallas as pl
from jax.experimental.pallas import tpu as pltpu
from jax.sharding import PartitionSpec as P

TILE = 128
STEPS = 4
POS = 16
LOWER = 6
GROUP = 2

learning_rate = 0.1
beta_rate = 0.9
pull_rate = 1.0

VMEM = pl.BlockSpec(memory_space=pltpu.VMEM)
SMEM = pl.BlockSpec(memory_space=pltpu.SMEM)
ANY = pl.BlockSpec(memory_space=pl.ANY)
MIB = 1024 * 1024


def select_kernel(n, which_ref, *refs):
    sources, outs = refs[:n], refs[n:]
    for k, out in enumerate(outs):
        for i, source in enumerate(sources):

            @pl.when(which_ref[k] == i)
            def _(source=source, out=out):
                out[...] = source[...]


def select(which, sources):
    size = sources[0].size * sources[0].dtype.itemsize
    return pl.pallas_call(
        functools.partial(select_kernel, len(sources)),
        out_shape=[pltpu.VMEM(sources[0].shape, sources[0].dtype)] * which.shape[0],
        in_specs=[SMEM] + [VMEM] * len(sources),
        out_specs=[VMEM] * which.shape[0],
        compiler_params=pltpu.CompilerParams(vmem_limit_bytes=12 * MIB),
        cost_estimate=pl.CostEstimate(
            flops=0, bytes_accessed=2 * which.shape[0] * size, transcendentals=0
        ),
        name="select_panels",
    )(which, *sources)


def pack_kernel(start, size, lab_ref, source, *refs):
    outs, sem = refs[:-1], refs[-1]
    n = len(outs)
    copies = []
    for k, out in enumerate(outs):
        piece = lax.rem(lab_ref[0] + k, n)
        row = pl.multiple_of(start + piece * size, 16)
        copies.append(pltpu.make_async_copy(source.at[pl.ds(row, size)], out, sem.at[k]))
    for copy in copies:
        copy.start()
    for copy in copies:
        copy.wait()


def pack(source, start, n, lab):
    size = (source.shape[0] - start) // n
    shape = (size, source.shape[1])
    return pl.pallas_call(
        functools.partial(pack_kernel, start, size),
        out_shape=[pltpu.VMEM(shape, source.dtype)] * n,
        in_specs=[SMEM, ANY],
        out_specs=[VMEM] * n,
        scratch_shapes=[pltpu.SemaphoreType.DMA((n,))],
        compiler_params=pltpu.CompilerParams(vmem_limit_bytes=8 * MIB),
        name="pack_pieces",
    )(lab, source)


def split(value):
    high = value.astype(jnp.bfloat16)
    return high, (value - high.astype(jnp.float32)).astype(jnp.bfloat16)


def product(pair, other, dims):
    dot = functools.partial(
        lax.dot_general, dimension_numbers=(dims, ((), ())), preferred_element_type=jnp.float32
    )
    return dot(pair[1], other) + dot(pair[0], other)


def update_kernel(first, top, size, offset, scale, group_ref, places_ref, panel_ref, *refs):
    n = places_ref.shape[0]
    pieces, refs = refs[:n], refs[n:]
    if first:
        live_ref, parents_ref, weight_ref, weight_out, moment_out, rows_ref = refs
    else:
        live_ref, parents_ref, weight_ref, moment_ref, weight_out, moment_out, rows_ref = refs
    labels, width = weight_ref.shape
    count = rows_ref.shape[0]
    rows_ref[:top, :] = panel_ref[:top, :]
    for k, piece in enumerate(pieces):
        row = pl.multiple_of(top + places_ref[k] * size, 16)
        rows_ref[pl.ds(row, size), :] = piece[offset : offset + size, :]
    rows = rows_ref[...]
    weight = weight_ref[...]
    pair = split(weight)
    group = group_ref[0].astype(jnp.bfloat16)
    within = panel_ref[top : top + POS, :count]
    own = jnp.where(panel_ref[top + POS :, :count] == group, within, jnp.bfloat16(-1.0))
    label = lax.broadcasted_iota(jnp.int32, (labels, count), 0)
    label = label.astype(jnp.float32).astype(jnp.bfloat16)
    target = jnp.zeros(label.shape, jnp.bfloat16)
    for k in range(POS):
        target = jnp.where(label == own[k : k + 1, :], jnp.bfloat16(1.0), target)
    scores = product(pair, rows, ((1,), (1,))) * scale
    resid = (jax.nn.sigmoid(scores) - target.astype(jnp.float32)) * live_ref[...]
    grad = product(split(resid), rows, ((1,), (0,)))
    column = lax.broadcasted_iota(jnp.int32, (labels, labels), 1)
    pick = (column == parents_ref[...]).astype(jnp.bfloat16)
    dot = functools.partial(jnp.dot, preferred_element_type=jnp.float32)
    parent = dot(pick, pair[1]) + dot(pick, pair[0])
    grad = grad * scale + pull_rate * (weight - parent)
    moment = grad if first else beta_rate * moment_ref[...] + grad
    moment_out[...] = moment
    weight_out[...] = weight - learning_rate * moment


def update(group, places, panel, pieces, offset, live, parents, weight, moment, last):
    labels, width = weight.shape
    count = live.shape[1]
    top = panel.shape[0] - 2 * POS
    size = (count - top) // len(pieces)
    first = moment is None
    state = [weight] if first else [weight, moment]
    shape = (jax.ShapeDtypeStruct if last else pltpu.VMEM)(weight.shape, jnp.float32)
    scale = 1.0 / float(width) ** 0.5
    return pl.pallas_call(
        functools.partial(update_kernel, first, top, size, offset, scale),
        out_shape=[shape, shape],
        in_specs=[SMEM, SMEM] + [VMEM] * (len(pieces) + 3 + len(state)),
        out_specs=[VMEM, VMEM],
        scratch_shapes=[pltpu.VMEM((count, width), panel.dtype)],
        compiler_params=pltpu.CompilerParams(vmem_limit_bytes=12 * MIB),
        cost_estimate=pl.CostEstimate(
            flops=8 * labels * width * count,
            bytes_accessed=2 * count * width + 16 * labels * width,
            transcendentals=labels * count,
        ),
        name="update_block",
    )(group, places, panel, *pieces, live, parents, *state)


def after(value, *earlier):
    return lax.optimization_barrier((value, *earlier))[0]


def circle(n):
    return [*range(0, 1), *range(1, n, 2), *reversed(range(2, n, 2))]


def send(what, value, axis, pairs, *earlier):
    value = after(value, *earlier) if earlier else value
    with jax.named_scope(what):
        return lax.ppermute(value, axis, pairs)


def local(embeddings, positives, weights, parents, owners, shortlist, counts):
    doc_index = lax.axis_index("doc")
    lab_index = lax.axis_index("lab")
    doc_count = lax.axis_size("doc")
    lab_count = lax.axis_size("lab")
    labels, width = weights.shape
    rows = embeddings.shape[0]
    home = doc_index * lab_count + lab_index
    unit = 16 * lab_count
    size = max(1, rows * LOWER // unit // 8) * 16
    top = rows - size * lab_count

    mine = pack(embeddings, top, lab_count, lab_index[None])

    groups = positives // labels
    codes = jnp.concatenate([positives - groups * labels, groups], axis=1).T
    codes = jnp.pad(codes, ((0, 0), (0, width - rows))).astype(jnp.bfloat16)
    upper = jnp.concatenate([embeddings[:top], codes], axis=0)

    order = circle(lab_count)
    order_of = jnp.array(order, jnp.int32)
    place_of = jnp.array([order.index(i) for i in range(lab_count)], jnp.int32)
    owner = lax.dynamic_index_in_dim(owners, doc_index, 1, keepdims=False)
    which_upper = (place_of[lab_index] - place_of[owner]) % lab_count
    which_lower = (lab_index - owner) % lab_count
    places = order_of[(place_of[lab_index] - jnp.arange(lab_count, dtype=jnp.int32)) % lab_count]
    lists = lax.dynamic_index_in_dim(shortlist, home, 1, keepdims=False)
    used = lax.dynamic_index_in_dim(counts, home, 1, keepdims=True)
    listed = lists[:, :, None] == jnp.arange(rows, dtype=jnp.int32) // TILE
    listed = listed & (jnp.arange(lists.shape[1], dtype=jnp.int32) < used)[:, :, None]
    live = jnp.any(listed, axis=1).astype(jnp.float32)
    group = jnp.arange(STEPS, dtype=jnp.int32)[:, None] * lab_count + lab_index
    parent_rows = lax.dynamic_slice_in_dim(parents, home * labels, labels, 0)[:, None]
    prepared = (which_upper, places, live, group, parent_rows)

    around = [(order[i], order[(i + 1) % lab_count]) for i in range(lab_count)]

    def shift(what, step, value, *earlier):
        pairs = [(i, (i - step) % doc_count) for i in range(doc_count)]
        return send(f"{what}_doc_shift_{step}", value, "doc", pairs, *earlier)

    met = [mine[0]]
    for k in range(1, lab_count):
        pairs = [(i, (i + k) % lab_count) for i in range(lab_count)]
        met.append(send(f"lower_lab_shift_{k}", mine[k], "lab", pairs))
    held = [upper]

    def hop(*earlier):
        held.append(send(f"upper_lab_hop_{len(held)}", held[-1], "lab", around, *earlier))

    hop(mine[0])
    lower = select(which_lower, met)
    hop(*prepared, lower[0])
    lower = [lower[0]] + [shift("lower", s, lower[s]) for s in range(1, STEPS)]
    for r in range(3, lab_count):
        hop(lower[1])
    parts = []
    for g in range(0, STEPS, GROUP):
        parts.append([jnp.concatenate(lower[g : g + GROUP], axis=0)])

    def spread(g, *earlier):
        part = parts[g]
        part.append(send(f"part_{g}_lab_hop_{len(part)}", part[-1], "lab", around, *earlier))

    spread(0)
    found = select(which_upper, [after(held[0], parts[0][1], *lower), *held[1:]])
    found = [found[0]] + [shift("upper", s, found[s]) for s in range(1, STEPS)]
    spread(1, found[0])
    for r in range(2, lab_count):
        spread(0, found[min(2 * r - 3, STEPS - 1)])
        spread(1, found[min(2 * r - 2, STEPS - 1)])

    weight, moment = weights, None
    for s in range(STEPS):
        weight, moment = update(
            group[s],
            places,
            found[s],
            parts[s // GROUP],
            s % GROUP * size,
            live[s : s + 1],
            parent_rows,
            weight,
            moment,
            s == STEPS - 1,
        )
    return (weight, moment)


def solution(mesh):
    return jax.shard_map(
        local,
        mesh=mesh,
        in_specs=(
            P(("doc", "lab"), None),
            P(("doc", "lab"), None),
            P(("doc", "lab"), None),
            P(),
            P(),
            P(),
            P(),
        ),
        out_specs=(P(("doc", "lab"), None), P(("doc", "lab"), None)),
        check_vma=False,
    )
```

```python
import functools

import jax
import jax.numpy as jnp
from jax import lax
from jax.experimental import pallas as pl
from jax.experimental.pallas import tpu as pltpu
from jax.sharding import PartitionSpec as P

TILE = 128
STEPS = 4
POS = 16
LOWER = 6
GROUPS = ((0, 1), (2, 3))
LANES = 128
UPDATE_MIB = 7
PACK_MIB = 48

learning_rate = 0.1
beta_rate = 0.9
pull_rate = 1.0

VMEM = pl.BlockSpec(memory_space=pltpu.VMEM)
SMEM = pl.BlockSpec(memory_space=pltpu.SMEM)
ANY = pl.BlockSpec(memory_space=pl.ANY)
MIB = 1024 * 1024


def select_kernel(n, which_ref, *refs):
    sources, outs = refs[:n], refs[n:]
    for k, out in enumerate(outs):
        for i, source in enumerate(sources):

            @pl.when(which_ref[k] == i)
            def _(source=source, out=out):
                out[...] = source[...]


def select(which, sources):
    size = sources[0].size * sources[0].dtype.itemsize
    return pl.pallas_call(
        functools.partial(select_kernel, len(sources)),
        out_shape=[pltpu.VMEM(sources[0].shape, sources[0].dtype)] * which.shape[0],
        in_specs=[SMEM] + [VMEM] * len(sources),
        out_specs=[VMEM] * which.shape[0],
        compiler_params=pltpu.CompilerParams(vmem_limit_bytes=12 * MIB),
        cost_estimate=pl.CostEstimate(
            flops=0, bytes_accessed=2 * which.shape[0] * size, transcendentals=0
        ),
        name="select_panels",
    )(which, *sources)


def pack_kernel(start, size, lab_ref, source, *refs):
    outs, sem = refs[:-1], refs[-1]
    n = len(outs)
    copies = []
    for k, out in enumerate(outs):
        piece = lax.rem(lab_ref[0] + k, n)
        row = pl.multiple_of(start + piece * size, 16)
        copies.append(pltpu.make_async_copy(source.at[pl.ds(row, size)], out, sem.at[k]))
    for copy in copies:
        copy.start()
    for copy in copies:
        copy.wait()


def pack(source, start, n, lab):
    size = (source.shape[0] - start) // n
    shape = (size, source.shape[1])
    return pl.pallas_call(
        functools.partial(pack_kernel, start, size),
        out_shape=[pltpu.VMEM(shape, source.dtype)] * n,
        in_specs=[SMEM, ANY],
        out_specs=[VMEM] * n,
        scratch_shapes=[pltpu.SemaphoreType.DMA((n,))],
        compiler_params=pltpu.CompilerParams(vmem_limit_bytes=PACK_MIB * MIB),
        name="pack_pieces",
    )(lab, source)


def coded(high, low):
    value = (low + 128).astype(jnp.float32) * 2.0**-64
    for bit in range(7):
        value = jnp.where((high >> bit) & 1 == 1, value * 2.0 ** (1 << bit), value)
    return value


def split(value):
    high = value.astype(jnp.bfloat16)
    return high, (value - high.astype(jnp.float32)).astype(jnp.bfloat16)


def product(pair, other, dims):
    dot = functools.partial(
        lax.dot_general, dimension_numbers=(dims, ((), ())), preferred_element_type=jnp.float32
    )
    return dot(pair[1], other) + dot(pair[0], other)


def update_kernel(first, top, size, offset, scale, places_ref, panel_ref, *refs):
    n = places_ref.shape[0]
    pieces, refs = refs[:n], refs[n:]
    if first:
        live_ref, pick_ref, weight_ref, weight_out, moment_out, rows_ref = refs
    else:
        live_ref, pick_ref, weight_ref, moment_ref, weight_out, moment_out, rows_ref = refs
    labels = weight_ref.shape[0]
    count = rows_ref.shape[0]
    rows_ref[:top, :] = panel_ref[:top, :]
    for k, piece in enumerate(pieces):
        row = pl.multiple_of(top + places_ref[k] * size, 16)
        rows_ref[pl.ds(row, size), :] = piece[offset : offset + size, :]
    rows = rows_ref[...]
    weight = weight_ref[...]
    pair = split(weight)
    label = lax.broadcasted_iota(jnp.int32, (labels, LANES), 0)
    label = ((label & 127) + 128) << (label >> 7)
    label = (label.astype(jnp.float32) * live_ref[:, count:]).astype(jnp.bfloat16)
    label = jnp.concatenate([label] * (count // LANES), axis=1)
    target = jnp.zeros(label.shape, jnp.bfloat16)
    for k in range(POS):
        code = panel_ref[top + k : top + k + 1, :count]
        target = jnp.where(label == code, jnp.bfloat16(1.0), target)
    scores = product(pair, rows, ((1,), (1,))) * scale
    resid = (jax.nn.sigmoid(scores) - target.astype(jnp.float32)) * live_ref[:, :count]
    grad = product(split(resid), rows, ((1,), (0,)))
    dot = functools.partial(jnp.dot, preferred_element_type=jnp.float32)
    parent = dot(pick_ref[...], pair[1]) + dot(pick_ref[...], pair[0])
    grad = grad * scale + pull_rate * (weight - parent)
    moment = grad if first else beta_rate * moment_ref[...] + grad
    moment_out[...] = moment
    weight_out[...] = weight - learning_rate * moment


def update(places, panel, pieces, offset, live, pick, weight, moment, last):
    labels, width = weight.shape
    count = live.shape[1] - LANES
    top = panel.shape[0] - POS
    size = (count - top) // len(pieces)
    first = moment is None
    state = [weight] if first else [weight, moment]
    shape = (jax.ShapeDtypeStruct if last else pltpu.VMEM)(weight.shape, jnp.float32)
    scale = 1.0 / float(width) ** 0.5
    return pl.pallas_call(
        functools.partial(update_kernel, first, top, size, offset, scale),
        out_shape=[shape, shape],
        in_specs=[SMEM] + [VMEM] * (len(pieces) + 3 + len(state)),
        out_specs=[VMEM, VMEM],
        scratch_shapes=[pltpu.VMEM((count, width), panel.dtype)],
        compiler_params=pltpu.CompilerParams(vmem_limit_bytes=UPDATE_MIB * MIB),
        cost_estimate=pl.CostEstimate(
            flops=8 * labels * width * count,
            bytes_accessed=2 * count * width + 16 * labels * width,
            transcendentals=labels * count,
        ),
        name="update_block",
    )(places, panel, *pieces, live, pick, *state)


def after(value, *earlier):
    return lax.optimization_barrier((value, *earlier))[0]


def circle(n):
    return [*range(0, 1), *range(1, n, 2), *reversed(range(2, n, 2))]


def send(what, value, axis, pairs, *earlier):
    value = after(value, *earlier) if earlier else value
    with jax.named_scope(what):
        return lax.ppermute(value, axis, pairs)


def local(embeddings, positives, weights, parents, owners, shortlist, counts):
    doc_index = lax.axis_index("doc")
    lab_index = lax.axis_index("lab")
    doc_count = lax.axis_size("doc")
    lab_count = lax.axis_size("lab")
    labels, width = weights.shape
    rows = embeddings.shape[0]
    home = doc_index * lab_count + lab_index
    grain = 16 * lab_count
    size = max(1, rows * LOWER // grain // 8) * 16
    top = rows - size * lab_count

    mine = pack(embeddings, top, lab_count, lab_index[None])

    codes = coded(positives.T >> 7, positives.T & 127).astype(jnp.bfloat16)
    codes = jnp.pad(codes, ((0, 0), (0, width - rows)))
    upper = jnp.concatenate([embeddings[:top], codes], axis=0)

    order = circle(lab_count)
    order_of = jnp.array(order, jnp.int32)
    place_of = jnp.array([order.index(i) for i in range(lab_count)], jnp.int32)
    owner = lax.dynamic_index_in_dim(owners, doc_index, 1, keepdims=False)
    which_upper = (place_of[lab_index] - place_of[owner]) % lab_count
    which_lower = (lab_index - owner) % lab_count
    places = order_of[(place_of[lab_index] - jnp.arange(lab_count, dtype=jnp.int32)) % lab_count]
    lists = lax.dynamic_index_in_dim(shortlist, home, 1, keepdims=False)
    used = lax.dynamic_index_in_dim(counts, home, 1, keepdims=True)
    listed = lists[:, :, None] == jnp.arange(rows, dtype=jnp.int32) // TILE
    listed = listed & (jnp.arange(lists.shape[1], dtype=jnp.int32) < used)[:, :, None]
    live = jnp.any(listed, axis=1).astype(jnp.float32)
    base = (jnp.arange(STEPS, dtype=jnp.int32) * lab_count + lab_index) * labels
    unit = jnp.broadcast_to(coded(base >> 7, jnp.zeros_like(base))[:, None], (STEPS, LANES))
    live = jnp.concatenate([live, unit / 128.0], axis=1)
    parent_rows = lax.dynamic_slice_in_dim(parents, home * labels, labels, 0)
    pick = parent_rows[:, None] == jnp.arange(labels, dtype=jnp.int32)
    pick = pick.astype(jnp.bfloat16)
    prepared = (which_upper, places, live, pick)

    around = [(order[i], order[(i + 1) % lab_count]) for i in range(lab_count)]

    def shift(what, step, value, *earlier):
        pairs = [(i, (i - step) % doc_count) for i in range(doc_count)]
        return send(f"{what}_doc_shift_{step}", value, "doc", pairs, *earlier)

    met = [mine[0]]
    for k in range(1, lab_count):
        pairs = [(i, (i + k) % lab_count) for i in range(lab_count)]
        met.append(send(f"lower_lab_shift_{k}", mine[k], "lab", pairs))
    held = [upper]

    def hop(*earlier):
        held.append(send(f"upper_lab_hop_{len(held)}", held[-1], "lab", around, *earlier))

    hop(mine[0])
    lower = select(which_lower, met)
    hop(*prepared, lower[0])
    lower = [lower[0]] + [shift("lower", s, lower[s]) for s in range(1, STEPS)]
    for r in range(3, lab_count):
        hop(*lower[1:])
    parts = [[jnp.concatenate([lower[s] for s in steps], axis=0)] for steps in GROUPS]

    def spread(g, *earlier):
        part = parts[g]
        part.append(send(f"part_{g}_lab_hop_{len(part)}", part[-1], "lab", around, *earlier))

    spread(0, *lower)
    found = select(which_upper, [after(held[0], parts[0][1]), *held[1:]])
    found = [found[0]] + [shift("upper", s, found[s]) for s in range(1, STEPS)]
    spread(1)
    for r in range(2, lab_count):
        if r == 2:
            spread(0)
        else:
            spread(0, found[min(r - 2, STEPS - 1)])
        spread(1, found[min(r - 1, STEPS - 1)])

    weight, moment = weights, None
    for s in range(STEPS):
        weight, moment = update(
            places,
            found[s],
            parts[s in GROUPS[1]],
            (s - GROUPS[s in GROUPS[1]][0]) * size,
            live[s : s + 1],
            pick,
            weight,
            moment,
            s == STEPS - 1,
        )
    return (weight, moment)


def solution(mesh):
    return jax.shard_map(
        local,
        mesh=mesh,
        in_specs=(
            P(("doc", "lab"), None),
            P(("doc", "lab"), None),
            P(("doc", "lab"), None),
            P(),
            P(),
            P(),
            P(),
        ),
        out_specs=(P(("doc", "lab"), None), P(("doc", "lab"), None)),
        check_vma=False,
    )
```

```python
import functools

import jax
import jax.numpy as jnp
from jax import lax
from jax.experimental import pallas as pl
from jax.experimental.pallas import tpu as pltpu
from jax.sharding import PartitionSpec as P

TILE = 128
STEPS = 4
POS = 16
LOWER = 6
GROUPS = ((0, 1), (2, 3))
LANES = 128
COLUMNS = 256
UPDATE_MIB = 7
PACK_MIB = 60

learning_rate = 0.1
beta_rate = 0.9
pull_rate = 1.0

VMEM = pl.BlockSpec(memory_space=pltpu.VMEM)
HBM = pl.BlockSpec(memory_space=pltpu.HBM)
MIB = 1024 * 1024


def circle(n):
    return [*range(0, 1), *range(1, n, 2), *reversed(range(2, n, 2))]


def select_kernel(n, which_ref, *refs):
    sources, outs = refs[:n], refs[n:]
    for k, out in enumerate(outs):
        which = which_ref[k : k + 1, :]
        value = sources[0][...]
        for i in range(1, n):
            value = jnp.where(which == jnp.bfloat16(i), sources[i][...], value)
        out[...] = value


def select(which, sources):
    size = sources[0].size * sources[0].dtype.itemsize
    count = which.shape[0]
    return pl.pallas_call(
        functools.partial(select_kernel, len(sources)),
        out_shape=[pltpu.VMEM(sources[0].shape, sources[0].dtype)] * count,
        in_specs=[VMEM] * (1 + len(sources)),
        out_specs=[VMEM] * count,
        compiler_params=pltpu.CompilerParams(vmem_limit_bytes=12 * MIB),
        cost_estimate=pl.CostEstimate(flops=0, bytes_accessed=2 * count * size, transcendentals=0),
        name="select_panels",
    )(which, *sources)


def pack_kernel(start, size, source, *refs):
    outs, sem = refs[:-1], refs[-1]
    n = len(outs)
    copies = []
    for k, out in enumerate(outs):
        piece = lax.rem(lax.axis_index("lab") + k, n)
        row = pl.multiple_of(start + piece * size, 16)
        copies.append(pltpu.make_async_copy(source.at[pl.ds(row, size)], out, sem.at[k]))
    for copy in copies:
        copy.start()
    for copy in copies:
        copy.wait()


def pack(source, start, n):
    size = (source.shape[0] - start) // n
    shape = (size, source.shape[1])
    return pl.pallas_call(
        functools.partial(pack_kernel, start, size),
        out_shape=[pltpu.VMEM(shape, source.dtype)] * n,
        in_specs=[HBM],
        out_specs=[VMEM] * n,
        scratch_shapes=[pltpu.SemaphoreType.DMA((n,))],
        compiler_params=pltpu.CompilerParams(vmem_limit_bytes=PACK_MIB * MIB),
        name="pack_pieces",
    )(source)


def coded(high, low):
    value = (low + 128).astype(jnp.float32) * 2.0**-64
    for bit in range(7):
        value = jnp.where((high >> bit) & 1 == 1, value * 2.0 ** (1 << bit), value)
    return value


def split(value):
    high = value.astype(jnp.bfloat16)
    return high, (value - high.astype(jnp.float32)).astype(jnp.bfloat16)


def product(pair, other, dims):
    dot = functools.partial(
        lax.dot_general, dimension_numbers=(dims, ((), ())), preferred_element_type=jnp.float32
    )
    return dot(pair[1], other) + dot(pair[0], other)


def update_kernel(first, last, n, top, size, offset, scale, panel_ref, *refs):
    order = circle(n)
    lab = lax.axis_index("lab")
    place = sum(jnp.where(lab == i, order.index(i), 0) for i in range(n))
    pieces, refs = refs[:n], refs[n:]
    live_ref, pick_ref, weight_ref, *refs = refs
    moment_ref = None if first else refs.pop(0)
    weight_out, moment_out, rows_ref, *refs = refs
    labels = weight_ref.shape[0]
    count = rows_ref.shape[0]
    rows_ref[:top, :] = panel_ref[:top, :]
    for k, piece in enumerate(pieces):
        at = lax.rem(place + n - k, n)
        plane = sum(jnp.where(at == i, order[i], 0) for i in range(n))
        row = pl.multiple_of(top + plane * size, 16)
        rows_ref[pl.ds(row, size), :] = piece[offset : offset + size, :]
    rows = rows_ref[...]
    weight = weight_ref[...]
    pair = split(weight)
    dot = functools.partial(jnp.dot, preferred_element_type=jnp.float32)
    parent = dot(pick_ref[...], pair[1]) + dot(pick_ref[...], pair[0])
    pull = pull_rate * (weight - parent)
    label = lax.broadcasted_iota(jnp.int32, (labels, LANES), 0)
    label = ((label & 127) + 128) << (label >> 7)
    label = (label.astype(jnp.float32) * live_ref[:, count:]).astype(jnp.bfloat16)
    label = jnp.concatenate([label] * (count // LANES), axis=1)
    target = jnp.zeros(label.shape, jnp.bfloat16)
    for k in range(POS):
        code = panel_ref[top + k : top + k + 1, :count]
        target = jnp.where(label == code, jnp.bfloat16(1.0), target)
    scores = product(pair, rows, ((1,), (1,))) * scale
    resid = (jax.nn.sigmoid(scores) - target.astype(jnp.float32)) * live_ref[:, :count]
    resid = split(resid)
    columns = COLUMNS if last else weight.shape[1]
    copies = []
    for c in range(0, weight.shape[1], columns):
        part = slice(c, c + columns)
        grad = product(resid, rows[:, part], ((1,), (0,))) * scale + pull[:, part]
        moment = grad if first else beta_rate * moment_ref[:, part] + grad
        value = weight[:, part] - learning_rate * moment
        if not last:
            moment_out[:, part] = moment
            weight_out[:, part] = value
            continue
        weight_held, moment_held, sem = refs
        weight_held[:, part] = value
        moment_held[:, part] = moment
        for held, out in ((weight_held, weight_out), (moment_held, moment_out)):
            done = sem.at[len(copies)]
            copies.append(pltpu.make_async_copy(held.at[:, part], out.at[:, part], done))
            copies[-1].start()
    for copy in copies:
        copy.wait()


def update(panel, pieces, offset, live, pick, weight, moment, last):
    labels, width = weight.shape
    count = live.shape[1] - LANES
    top = panel.shape[0] - POS
    size = (count - top) // len(pieces)
    first = moment is None
    state = [weight] if first else [weight, moment]
    shape = (jax.ShapeDtypeStruct if last else pltpu.VMEM)(weight.shape, jnp.float32)
    scratch = [pltpu.VMEM((count, width), panel.dtype)]
    if last:
        scratch += [pltpu.VMEM(weight.shape, jnp.float32)] * 2
        scratch += [pltpu.SemaphoreType.DMA((2 * width // COLUMNS,))]
    scale = 1.0 / float(width) ** 0.5
    return pl.pallas_call(
        functools.partial(update_kernel, first, last, len(pieces), top, size, offset, scale),
        out_shape=[shape, shape],
        in_specs=[VMEM] * (len(pieces) + 3 + len(state)),
        out_specs=[HBM if last else VMEM] * 2,
        scratch_shapes=scratch,
        compiler_params=pltpu.CompilerParams(vmem_limit_bytes=UPDATE_MIB * MIB),
        cost_estimate=pl.CostEstimate(
            flops=8 * labels * width * count,
            bytes_accessed=2 * count * width + 16 * labels * width,
            transcendentals=labels * count,
        ),
        name="update_block",
    )(panel, *pieces, live, pick, *state)


def after(value, *earlier):
    return lax.optimization_barrier((value, *earlier))[0]


def send(what, value, axis, pairs, *earlier):
    value = after(value, *earlier) if earlier else value
    with jax.named_scope(what):
        return lax.ppermute(value, axis, pairs)


def local(embeddings, positives, weights, parents, owners, shortlist, counts):
    doc_index = lax.axis_index("doc")
    lab_index = lax.axis_index("lab")
    doc_count = lax.axis_size("doc")
    lab_count = lax.axis_size("lab")
    labels, width = weights.shape
    rows = embeddings.shape[0]
    home = doc_index * lab_count + lab_index
    grain = 16 * lab_count
    size = max(1, rows * LOWER // grain // 8) * 16
    top = rows - size * lab_count

    mine = pack(embeddings, top, lab_count)

    codes = coded(positives.T >> 7, positives.T & 127).astype(jnp.bfloat16)
    codes = jnp.pad(codes, ((0, 0), (0, width - rows)))
    upper = jnp.concatenate([embeddings[:top], codes], axis=0)

    order = circle(lab_count)
    place_of = jnp.array([order.index(i) for i in range(lab_count)], jnp.int32)
    owner = lax.dynamic_index_in_dim(owners, doc_index, 1, keepdims=False)
    which_upper = (place_of[lab_index] - place_of[owner]) % lab_count
    which_lower = (lab_index - owner) % lab_count
    which_upper, which_lower = (
        jnp.broadcast_to(which[:, None], (STEPS, width)).astype(jnp.bfloat16)
        for which in (which_upper, which_lower)
    )
    lists = lax.dynamic_index_in_dim(shortlist, home, 1, keepdims=False)
    used = lax.dynamic_index_in_dim(counts, home, 1, keepdims=True)
    listed = lists[:, :, None] == jnp.arange(rows, dtype=jnp.int32) // TILE
    listed = listed & (jnp.arange(lists.shape[1], dtype=jnp.int32) < used)[:, :, None]
    live = jnp.any(listed, axis=1).astype(jnp.float32)
    base = (jnp.arange(STEPS, dtype=jnp.int32) * lab_count + lab_index) * labels
    unit = jnp.broadcast_to(coded(base >> 7, jnp.zeros_like(base))[:, None], (STEPS, LANES))
    live = jnp.concatenate([live, unit / 128.0], axis=1)
    parent_rows = lax.dynamic_slice_in_dim(parents, home * labels, labels, 0)
    pick = parent_rows[:, None] == jnp.arange(labels, dtype=jnp.int32)
    pick = pick.astype(jnp.bfloat16)
    prepared = (which_upper, live, pick)

    around = [(order[i], order[(i + 1) % lab_count]) for i in range(lab_count)]

    def shift(what, step, value, *earlier):
        pairs = [(i, (i - step) % doc_count) for i in range(doc_count)]
        return send(f"{what}_doc_shift_{step}", value, "doc", pairs, *earlier)

    met = [mine[0]]
    for k in range(1, lab_count):
        pairs = [(i, (i + k) % lab_count) for i in range(lab_count)]
        met.append(send(f"lower_lab_shift_{k}", mine[k], "lab", pairs))
    held = [upper]

    def hop(*earlier):
        held.append(send(f"upper_lab_hop_{len(held)}", held[-1], "lab", around, *earlier))

    hop(mine[0])
    lower = select(which_lower, met)
    hop(*prepared, lower[0])
    lower = [lower[0]] + [shift("lower", s, lower[s]) for s in range(1, STEPS)]
    for r in range(3, lab_count):
        hop(*lower[1:])
    parts = [[jnp.concatenate([lower[s] for s in steps], axis=0)] for steps in GROUPS]

    def spread(g, *earlier):
        part = parts[g]
        part.append(send(f"part_{g}_lab_hop_{len(part)}", part[-1], "lab", around, *earlier))

    spread(0, *lower)
    found = select(which_upper, [after(held[0], parts[0][1]), *held[1:]])
    found = [found[0]] + [shift("upper", s, found[s]) for s in range(1, STEPS)]
    spread(1)
    for r in range(2, lab_count):
        if r == 2:
            spread(0)
        else:
            spread(0, found[min(r - 2, STEPS - 1)])
        spread(1, found[min(r - 1, STEPS - 1)])

    weight, moment = weights, None
    for s in range(STEPS):
        weight, moment = update(
            found[s],
            parts[s in GROUPS[1]],
            (s - GROUPS[s in GROUPS[1]][0]) * size,
            live[s : s + 1],
            pick,
            weight,
            moment,
            s == STEPS - 1,
        )
    return (weight, moment)


def solution(mesh):
    return jax.shard_map(
        local,
        mesh=mesh,
        in_specs=(
            P(("doc", "lab"), None),
            P(("doc", "lab"), None),
            P(("doc", "lab"), None),
            P(),
            P(),
            P(),
            P(),
        ),
        out_specs=(P(("doc", "lab"), None), P(("doc", "lab"), None)),
        check_vma=False,
    )
```

```python
import functools

import jax
import jax.numpy as jnp
from jax import lax
from jax.experimental import pallas as pl
from jax.experimental.pallas import tpu as pltpu
from jax.sharding import PartitionSpec as P

TILE = 128
STEPS = 4
POS = 16
LOWER = 5
GROUPS = ((0, 1), (2, 3))
LANES = 128
COLUMNS = 256
UPDATE_MIB = 7
PACK_MIB = 60

learning_rate = 0.1
beta_rate = 0.9
pull_rate = 1.0

VMEM = pl.BlockSpec(memory_space=pltpu.VMEM)
HBM = pl.BlockSpec(memory_space=pltpu.HBM)
MIB = 1024 * 1024


def circle(n):
    return [*range(0, 1), *range(1, n, 2), *reversed(range(2, n, 2))]


def select_kernel(n, which_ref, *refs):
    sources, outs = refs[:n], refs[n:]
    for k, out in enumerate(outs):
        which = which_ref[k : k + 1, :]
        value = sources[0][...]
        for i in range(1, n):
            value = jnp.where(which == jnp.bfloat16(i), sources[i][...], value)
        out[...] = value


def select(which, sources):
    size = sources[0].size * sources[0].dtype.itemsize
    count = which.shape[0]
    return pl.pallas_call(
        functools.partial(select_kernel, len(sources)),
        out_shape=[pltpu.VMEM(sources[0].shape, sources[0].dtype)] * count,
        in_specs=[VMEM] * (1 + len(sources)),
        out_specs=[VMEM] * count,
        compiler_params=pltpu.CompilerParams(vmem_limit_bytes=12 * MIB),
        cost_estimate=pl.CostEstimate(flops=0, bytes_accessed=2 * count * size, transcendentals=0),
        name="select_panels",
    )(which, *sources)


def pack_kernel(start, size, source, *refs):
    outs, sem = refs[:-1], refs[-1]
    n = len(outs)
    copies = []
    for k, out in enumerate(outs):
        piece = lax.rem(lax.axis_index("lab") + k, n)
        row = pl.multiple_of(start + piece * size, 16)
        copies.append(pltpu.make_async_copy(source.at[pl.ds(row, size)], out, sem.at[k]))
    for copy in copies:
        copy.start()
    for copy in copies:
        copy.wait()


def pack(source, start, n):
    size = (source.shape[0] - start) // n
    shape = (size, source.shape[1])
    return pl.pallas_call(
        functools.partial(pack_kernel, start, size),
        out_shape=[pltpu.VMEM(shape, source.dtype)] * n,
        in_specs=[HBM],
        out_specs=[VMEM] * n,
        scratch_shapes=[pltpu.SemaphoreType.DMA((n,))],
        compiler_params=pltpu.CompilerParams(vmem_limit_bytes=PACK_MIB * MIB),
        name="pack_pieces",
    )(source)


def coded(high, low):
    value = (low + 128).astype(jnp.float32) * 2.0**-64
    for bit in range(7):
        value = jnp.where((high >> bit) & 1 == 1, value * 2.0 ** (1 << bit), value)
    return value


def split(value):
    high = value.astype(jnp.bfloat16)
    return high, (value - high.astype(jnp.float32)).astype(jnp.bfloat16)


def product(pair, other, dims):
    dot = functools.partial(
        lax.dot_general, dimension_numbers=(dims, ((), ())), preferred_element_type=jnp.float32
    )
    return dot(pair[1], other) + dot(pair[0], other)


def update_kernel(first, last, n, top, size, offset, scale, panel_ref, *refs):
    order = circle(n)
    lab = lax.axis_index("lab")
    place = sum(jnp.where(lab == i, order.index(i), 0) for i in range(n))
    pieces, refs = refs[:n], refs[n:]
    live_ref, pick_ref, weight_ref, *refs = refs
    moment_ref = None if first else refs.pop(0)
    weight_out, moment_out, rows_ref, *refs = refs
    labels = weight_ref.shape[0]
    count = rows_ref.shape[0]
    rows_ref[:top, :] = panel_ref[:top, :]
    for k, piece in enumerate(pieces):
        at = lax.rem(place + n - k, n)
        plane = sum(jnp.where(at == i, order[i], 0) for i in range(n))
        row = pl.multiple_of(top + plane * size, 16)
        rows_ref[pl.ds(row, size), :] = piece[offset : offset + size, :]
    rows = rows_ref[...]
    weight = weight_ref[...]
    pair = split(weight)
    dot = functools.partial(jnp.dot, preferred_element_type=jnp.float32)
    parent = dot(pick_ref[...], pair[1]) + dot(pick_ref[...], pair[0])
    pull = pull_rate * (weight - parent)
    label = lax.broadcasted_iota(jnp.int32, (labels, LANES), 0)
    label = ((label & 127) + 128) << (label >> 7)
    label = (label.astype(jnp.float32) * live_ref[:, count:]).astype(jnp.bfloat16)
    label = jnp.concatenate([label] * (count // LANES), axis=1)
    target = jnp.zeros(label.shape, jnp.bfloat16)
    for k in range(POS):
        code = panel_ref[top + k : top + k + 1, :count]
        target = jnp.where(label == code, jnp.bfloat16(1.0), target)
    scores = product(pair, rows, ((1,), (1,))) * scale
    resid = (jax.nn.sigmoid(scores) - target.astype(jnp.float32)) * live_ref[:, :count]
    resid = split(resid)
    columns = COLUMNS if last else weight.shape[1]
    copies = []
    for c in range(0, weight.shape[1], columns):
        part = slice(c, c + columns)
        grad = product(resid, rows[:, part], ((1,), (0,))) * scale + pull[:, part]
        moment = grad if first else beta_rate * moment_ref[:, part] + grad
        value = weight[:, part] - learning_rate * moment
        if not last:
            moment_out[:, part] = moment
            weight_out[:, part] = value
            continue
        weight_held, moment_held, sem = refs
        weight_held[:, part] = value
        moment_held[:, part] = moment
        for held, out in ((weight_held, weight_out), (moment_held, moment_out)):
            done = sem.at[len(copies)]
            copies.append(pltpu.make_async_copy(held.at[:, part], out.at[:, part], done))
            copies[-1].start()
    for copy in copies:
        copy.wait()


def update(panel, pieces, offset, live, pick, weight, moment, last):
    labels, width = weight.shape
    count = live.shape[1] - LANES
    top = panel.shape[0] - POS
    size = (count - top) // len(pieces)
    first = moment is None
    state = [weight] if first else [weight, moment]
    shape = (jax.ShapeDtypeStruct if last else pltpu.VMEM)(weight.shape, jnp.float32)
    scratch = [pltpu.VMEM((count, width), panel.dtype)]
    if last:
        scratch += [pltpu.VMEM(weight.shape, jnp.float32)] * 2
        scratch += [pltpu.SemaphoreType.DMA((2 * width // COLUMNS,))]
    scale = 1.0 / float(width) ** 0.5
    return pl.pallas_call(
        functools.partial(update_kernel, first, last, len(pieces), top, size, offset, scale),
        out_shape=[shape, shape],
        in_specs=[VMEM] * (len(pieces) + 3 + len(state)),
        out_specs=[HBM if last else VMEM] * 2,
        scratch_shapes=scratch,
        compiler_params=pltpu.CompilerParams(vmem_limit_bytes=UPDATE_MIB * MIB),
        cost_estimate=pl.CostEstimate(
            flops=8 * labels * width * count,
            bytes_accessed=2 * count * width + 16 * labels * width,
            transcendentals=labels * count,
        ),
        name="update_block",
    )(panel, *pieces, live, pick, *state)


def after(value, *earlier):
    return lax.optimization_barrier((value, *earlier))[0]


def send(what, value, axis, pairs, *earlier):
    value = after(value, *earlier) if earlier else value
    with jax.named_scope(what):
        return lax.ppermute(value, axis, pairs)


def local(embeddings, positives, weights, parents, owners, shortlist, counts):
    doc_index = lax.axis_index("doc")
    lab_index = lax.axis_index("lab")
    doc_count = lax.axis_size("doc")
    lab_count = lax.axis_size("lab")
    labels, width = weights.shape
    rows = embeddings.shape[0]
    home = doc_index * lab_count + lab_index
    grain = 16 * lab_count
    size = max(1, rows * LOWER // grain // 8) * 16
    top = rows - size * lab_count

    mine = pack(embeddings, top, lab_count)

    codes = coded(positives.T >> 7, positives.T & 127).astype(jnp.bfloat16)
    codes = jnp.pad(codes, ((0, 0), (0, width - rows)))
    upper = jnp.concatenate([embeddings[:top], codes], axis=0)

    order = circle(lab_count)
    place_of = jnp.array([order.index(i) for i in range(lab_count)], jnp.int32)
    owner = lax.dynamic_index_in_dim(owners, doc_index, 1, keepdims=False)
    which_upper = (place_of[lab_index] - place_of[owner]) % lab_count
    which_lower = (lab_index - owner) % lab_count
    which_upper, which_lower = (
        jnp.broadcast_to(which[:, None], (STEPS, width)).astype(jnp.bfloat16)
        for which in (which_upper, which_lower)
    )
    lists = lax.dynamic_index_in_dim(shortlist, home, 1, keepdims=False)
    used = lax.dynamic_index_in_dim(counts, home, 1, keepdims=True)
    listed = lists[:, :, None] == jnp.arange(rows, dtype=jnp.int32) // TILE
    listed = listed & (jnp.arange(lists.shape[1], dtype=jnp.int32) < used)[:, :, None]
    live = jnp.any(listed, axis=1).astype(jnp.float32)
    base = (jnp.arange(STEPS, dtype=jnp.int32) * lab_count + lab_index) * labels
    unit = jnp.broadcast_to(coded(base >> 7, jnp.zeros_like(base))[:, None], (STEPS, LANES))
    live = jnp.concatenate([live, unit / 128.0], axis=1)
    parent_rows = lax.dynamic_slice_in_dim(parents, home * labels, labels, 0)
    pick = parent_rows[:, None] == jnp.arange(labels, dtype=jnp.int32)
    pick = pick.astype(jnp.bfloat16)
    prepared = (which_upper, live, pick)

    around = [(order[i], order[(i + 1) % lab_count]) for i in range(lab_count)]

    def shift(what, step, value, *earlier):
        pairs = [(i, (i - step) % doc_count) for i in range(doc_count)]
        return send(f"{what}_doc_shift_{step}", value, "doc", pairs, *earlier)

    met = [mine[0]]
    for k in range(1, lab_count):
        pairs = [(i, (i + k) % lab_count) for i in range(lab_count)]
        met.append(send(f"lower_lab_shift_{k}", mine[k], "lab", pairs))
    held = [upper]

    def hop(*earlier):
        held.append(send(f"upper_lab_hop_{len(held)}", held[-1], "lab", around, *earlier))

    hop(mine[0])
    lower = select(which_lower, met)
    hop(*prepared, lower[0])
    lower = [lower[0]] + [shift("lower", s, lower[s]) for s in range(1, STEPS)]
    for r in range(3, lab_count):
        hop(*lower[1:])
    parts = [[jnp.concatenate([lower[s] for s in steps], axis=0)] for steps in GROUPS]

    def spread(g, *earlier):
        part = parts[g]
        part.append(send(f"part_{g}_lab_hop_{len(part)}", part[-1], "lab", around, *earlier))

    spread(0, *lower[1:])
    found = select(which_upper, [after(held[0], parts[0][1]), *held[1:]])
    found = [found[0]] + [shift("upper", s, found[s]) for s in range(1, STEPS)]
    spread(1)
    for r in range(2, lab_count):
        spread(0)
        spread(1, found[0 if r == 2 else 2])

    weight, moment = weights, None
    for s in range(STEPS):
        weight, moment = update(
            found[s],
            parts[s in GROUPS[1]],
            (s - GROUPS[s in GROUPS[1]][0]) * size,
            live[s : s + 1],
            pick,
            weight,
            moment,
            s == STEPS - 1,
        )
    return (weight, moment)


def solution(mesh):
    return jax.shard_map(
        local,
        mesh=mesh,
        in_specs=(
            P(("doc", "lab"), None),
            P(("doc", "lab"), None),
            P(("doc", "lab"), None),
            P(),
            P(),
            P(),
            P(),
        ),
        out_specs=(P(("doc", "lab"), None), P(("doc", "lab"), None)),
        check_vma=False,
    )
```

```python
import functools

import jax
import jax.numpy as jnp
from jax import lax
from jax.experimental import pallas as pl
from jax.experimental.pallas import tpu as pltpu
from jax.sharding import PartitionSpec as P

TILE = 128
STEPS = 4
POS = 16
LOWER = 4
GROUPS = ((0, 1), (2, 3))
LANES = 128
COLUMNS = 256
UPDATE_MIB = 7
PACK_MIB = 60

learning_rate = 0.1
beta_rate = 0.9
pull_rate = 1.0

VMEM = pl.BlockSpec(memory_space=pltpu.VMEM)
HBM = pl.BlockSpec(memory_space=pltpu.HBM)
MIB = 1024 * 1024


def circle(n):
    return [*range(0, 1), *range(1, n, 2), *reversed(range(2, n, 2))]


def select_kernel(n, which_ref, *refs):
    sources, outs = refs[:n], refs[n:]
    for k, out in enumerate(outs):
        which = which_ref[k : k + 1, :]
        value = sources[0][...]
        for i in range(1, n):
            value = jnp.where(which == jnp.bfloat16(i), sources[i][...], value)
        out[...] = value


def select(which, sources):
    size = sources[0].size * sources[0].dtype.itemsize
    count = which.shape[0]
    return pl.pallas_call(
        functools.partial(select_kernel, len(sources)),
        out_shape=[pltpu.VMEM(sources[0].shape, sources[0].dtype)] * count,
        in_specs=[VMEM] * (1 + len(sources)),
        out_specs=[VMEM] * count,
        compiler_params=pltpu.CompilerParams(vmem_limit_bytes=12 * MIB),
        cost_estimate=pl.CostEstimate(flops=0, bytes_accessed=2 * count * size, transcendentals=0),
        name="select_panels",
    )(which, *sources)


def pack_kernel(start, size, source, *refs):
    outs, sem = refs[:-1], refs[-1]
    n = len(outs)
    copies = []
    for k, out in enumerate(outs):
        piece = lax.rem(lax.axis_index("lab") + k, n)
        row = pl.multiple_of(start + piece * size, 16)
        copies.append(pltpu.make_async_copy(source.at[pl.ds(row, size)], out, sem.at[k]))
    for copy in copies:
        copy.start()
    for copy in copies:
        copy.wait()


def pack(source, start, n):
    size = (source.shape[0] - start) // n
    shape = (size, source.shape[1])
    return pl.pallas_call(
        functools.partial(pack_kernel, start, size),
        out_shape=[pltpu.VMEM(shape, source.dtype)] * n,
        in_specs=[HBM],
        out_specs=[VMEM] * n,
        scratch_shapes=[pltpu.SemaphoreType.DMA((n,))],
        compiler_params=pltpu.CompilerParams(vmem_limit_bytes=PACK_MIB * MIB),
        name="pack_pieces",
    )(source)


def coded(high, low):
    value = (low + 128).astype(jnp.float32) * 2.0**-64
    for bit in range(7):
        value = jnp.where((high >> bit) & 1 == 1, value * 2.0 ** (1 << bit), value)
    return value


def split(value):
    high = value.astype(jnp.bfloat16)
    return high, (value - high.astype(jnp.float32)).astype(jnp.bfloat16)


def product(pair, other, dims):
    dot = functools.partial(
        lax.dot_general, dimension_numbers=(dims, ((), ())), preferred_element_type=jnp.float32
    )
    return dot(pair[1], other) + dot(pair[0], other)


def update_kernel(first, last, n, tops, size, offset, scale, *refs):
    order = circle(n)
    lab = lax.axis_index("lab")
    place = sum(jnp.where(lab == i, order.index(i), 0) for i in range(n))
    panels, refs = refs[: len(tops)], refs[len(tops) :]
    pieces, refs = refs[:n], refs[n:]
    live_ref, pick_ref, weight_ref, *refs = refs
    moment_ref = None if first else refs.pop(0)
    weight_out, moment_out, rows_ref, *refs = refs
    labels = weight_ref.shape[0]
    count = rows_ref.shape[0]
    top = 0
    for panel_ref, rows in zip(panels, tops):
        rows_ref[top : top + rows, :] = panel_ref[:rows, :]
        top += rows
    for k, piece in enumerate(pieces):
        at = lax.rem(place + n - k, n)
        plane = sum(jnp.where(at == i, order[i], 0) for i in range(n))
        row = pl.multiple_of(top + plane * size, 16)
        rows_ref[pl.ds(row, size), :] = piece[offset : offset + size, :]
    rows = rows_ref[...]
    weight = weight_ref[...]
    pair = split(weight)
    dot = functools.partial(jnp.dot, preferred_element_type=jnp.float32)
    parent = dot(pick_ref[...], pair[1]) + dot(pick_ref[...], pair[0])
    pull = pull_rate * (weight - parent)
    label = lax.broadcasted_iota(jnp.int32, (labels, LANES), 0)
    label = ((label & 127) + 128) << (label >> 7)
    label = (label.astype(jnp.float32) * live_ref[:, count:]).astype(jnp.bfloat16)
    label = jnp.concatenate([label] * (count // LANES), axis=1)
    target = jnp.zeros(label.shape, jnp.bfloat16)
    for k in range(POS):
        code = panels[0][tops[0] + k : tops[0] + k + 1, :count]
        target = jnp.where(label == code, jnp.bfloat16(1.0), target)
    scores = product(pair, rows, ((1,), (1,))) * scale
    resid = (jax.nn.sigmoid(scores) - target.astype(jnp.float32)) * live_ref[:, :count]
    resid = split(resid)
    columns = COLUMNS if last else weight.shape[1]
    copies = []
    for c in range(0, weight.shape[1], columns):
        part = slice(c, c + columns)
        grad = product(resid, rows[:, part], ((1,), (0,))) * scale + pull[:, part]
        moment = grad if first else beta_rate * moment_ref[:, part] + grad
        value = weight[:, part] - learning_rate * moment
        if not last:
            moment_out[:, part] = moment
            weight_out[:, part] = value
            continue
        weight_held, moment_held, sem = refs
        weight_held[:, part] = value
        moment_held[:, part] = moment
        for held, out in ((weight_held, weight_out), (moment_held, moment_out)):
            done = sem.at[len(copies)]
            copies.append(pltpu.make_async_copy(held.at[:, part], out.at[:, part], done))
            copies[-1].start()
    for copy in copies:
        copy.wait()


def update(panels, pieces, offset, live, pick, weight, moment, last):
    labels, width = weight.shape
    count = live.shape[1] - LANES
    tops = [panel.shape[0] for panel in panels]
    tops[0] -= POS
    size = (count - sum(tops)) // len(pieces)
    first = moment is None
    state = [weight] if first else [weight, moment]
    shape = (jax.ShapeDtypeStruct if last else pltpu.VMEM)(weight.shape, jnp.float32)
    scratch = [pltpu.VMEM((count, width), panels[0].dtype)]
    if last:
        scratch += [pltpu.VMEM(weight.shape, jnp.float32)] * 2
        scratch += [pltpu.SemaphoreType.DMA((2 * width // COLUMNS,))]
    scale = 1.0 / float(width) ** 0.5
    return pl.pallas_call(
        functools.partial(update_kernel, first, last, len(pieces), tops, size, offset, scale),
        out_shape=[shape, shape],
        in_specs=[VMEM] * (len(panels) + len(pieces) + 2 + len(state)),
        out_specs=[HBM if last else VMEM] * 2,
        scratch_shapes=scratch,
        compiler_params=pltpu.CompilerParams(vmem_limit_bytes=UPDATE_MIB * MIB),
        cost_estimate=pl.CostEstimate(
            flops=8 * labels * width * count,
            bytes_accessed=2 * count * width + 16 * labels * width,
            transcendentals=labels * count,
        ),
        name="update_block",
    )(*panels, *pieces, live, pick, *state)


def after(value, *earlier):
    return lax.optimization_barrier((value, *earlier))[0]


def send(what, value, axis, pairs, *earlier):
    value = after(value, *earlier) if earlier else value
    with jax.named_scope(what):
        return lax.ppermute(value, axis, pairs)


def local(embeddings, positives, weights, parents, owners, shortlist, counts):
    doc_index = lax.axis_index("doc")
    lab_index = lax.axis_index("lab")
    doc_count = lax.axis_size("doc")
    lab_count = lax.axis_size("lab")
    labels, width = weights.shape
    rows = embeddings.shape[0]
    home = doc_index * lab_count + lab_index
    grain = 16 * lab_count
    size = max(1, rows * LOWER // grain // 8) * 16
    top = rows - size * lab_count

    mine = pack(embeddings, top, lab_count)

    codes = coded(positives.T >> 7, positives.T & 127).astype(jnp.bfloat16)
    codes = jnp.pad(codes, ((0, 0), (0, width - rows)))
    first = top // 32 * 16
    upper = [jnp.concatenate([embeddings[:first], codes], axis=0), embeddings[first:top]]

    order = circle(lab_count)
    place_of = jnp.array([order.index(i) for i in range(lab_count)], jnp.int32)
    owner = lax.dynamic_index_in_dim(owners, doc_index, 1, keepdims=False)
    which_upper = (place_of[lab_index] - place_of[owner]) % lab_count
    which_lower = (lab_index - owner) % lab_count
    which_upper, which_lower = (
        jnp.broadcast_to(which[:, None], (STEPS, width)).astype(jnp.bfloat16)
        for which in (which_upper, which_lower)
    )
    lists = lax.dynamic_index_in_dim(shortlist, home, 1, keepdims=False)
    used = lax.dynamic_index_in_dim(counts, home, 1, keepdims=True)
    listed = lists[:, :, None] == jnp.arange(rows, dtype=jnp.int32) // TILE
    listed = listed & (jnp.arange(lists.shape[1], dtype=jnp.int32) < used)[:, :, None]
    live = jnp.any(listed, axis=1).astype(jnp.float32)
    base = (jnp.arange(STEPS, dtype=jnp.int32) * lab_count + lab_index) * labels
    unit = jnp.broadcast_to(coded(base >> 7, jnp.zeros_like(base))[:, None], (STEPS, LANES))
    live = jnp.concatenate([live, unit / 128.0], axis=1)
    parent_rows = lax.dynamic_slice_in_dim(parents, home * labels, labels, 0)
    pick = parent_rows[:, None] == jnp.arange(labels, dtype=jnp.int32)
    pick = pick.astype(jnp.bfloat16)
    prepared = (which_upper, live, pick)

    around = [(order[i], order[(i + 1) % lab_count]) for i in range(lab_count)]

    def shift(what, step, value, *earlier):
        pairs = [(i, (i - step) % doc_count) for i in range(doc_count)]
        return send(f"{what}_doc_shift_{step}", value, "doc", pairs, *earlier)

    met = [mine[0]]
    for k in range(1, lab_count):
        pairs = [(i, (i + k) % lab_count) for i in range(lab_count)]
        met.append(send(f"lower_lab_shift_{k}", mine[k], "lab", pairs))
    held = [[chunk] for chunk in upper]

    def hop(what, line, *earlier):
        line.append(send(f"{what}_lab_hop_{len(line)}", line[-1], "lab", around, *earlier))

    hop("upper_0", held[0], mine[0])
    hop("upper_1", held[1], mine[0])
    lower = select(which_lower, met)
    hop("upper_0", held[0], *prepared, lower[0])
    lower = [lower[0]] + [shift("lower", s, lower[s]) for s in range(1, STEPS)]
    parts = [[jnp.concatenate([lower[s] for s in steps], axis=0)] for steps in GROUPS]
    hop("upper_1", held[1], held[0][2])
    for r in range(3, lab_count):
        hop("upper_0", held[0], *lower[1:])
    hop("part_0", parts[0], *lower[1:])
    ahead = select(which_upper, held[0])
    panels = [[ahead[0]]] + [[shift("upper_0", s, ahead[s])] for s in range(1, STEPS)]
    for r in range(3, lab_count):
        hop("upper_1", held[1], ahead[0])
    hop("part_1", parts[1])
    found = select(which_upper, held[1])
    panels[0].append(found[0])
    for s in range(1, STEPS):
        panels[s].append(shift("upper_1", s, found[s], panels[s][0]))
    for r in range(2, lab_count):
        hop("part_0", parts[0], *(panels[2][:1] if r > 2 else ()))
        hop("part_1", parts[1], panels[1 if r == 2 else 2][0])

    weight, moment = weights, None
    for s in range(STEPS):
        weight, moment = update(
            panels[s],
            parts[s in GROUPS[1]],
            (s - GROUPS[s in GROUPS[1]][0]) * size,
            live[s : s + 1],
            pick,
            weight,
            moment,
            s == STEPS - 1,
        )
    return (weight, moment)


def solution(mesh):
    return jax.shard_map(
        local,
        mesh=mesh,
        in_specs=(
            P(("doc", "lab"), None),
            P(("doc", "lab"), None),
            P(("doc", "lab"), None),
            P(),
            P(),
            P(),
            P(),
        ),
        out_specs=(P(("doc", "lab"), None), P(("doc", "lab"), None)),
        check_vma=False,
    )
```

```python
import functools

import jax
import jax.numpy as jnp
from jax import lax
from jax.experimental import pallas as pl
from jax.experimental.pallas import tpu as pltpu
from jax.sharding import PartitionSpec as P

TILE = 128
STEPS = 4
POS = 16
LOWER = 4
GROUPS = ((0, 1), (2, 3))
LANES = 128
COLUMNS = 256
UPDATE_MIB = 7
PACK_MIB = 60

learning_rate = 0.1
beta_rate = 0.9
pull_rate = 1.0

VMEM = pl.BlockSpec(memory_space=pltpu.VMEM)
HBM = pl.BlockSpec(memory_space=pltpu.HBM)
MIB = 1024 * 1024


def circle(n):
    return [*range(0, 1), *range(1, n, 2), *reversed(range(2, n, 2))]


def select_kernel(n, which_ref, *refs):
    sources, outs = refs[:n], refs[n:]
    for k, out in enumerate(outs):
        which = which_ref[k : k + 1, :]
        value = sources[0][...]
        for i in range(1, n):
            value = jnp.where(which == jnp.bfloat16(i), sources[i][...], value)
        out[...] = value


def select(which, sources):
    size = sources[0].size * sources[0].dtype.itemsize
    count = which.shape[0]
    return pl.pallas_call(
        functools.partial(select_kernel, len(sources)),
        out_shape=[pltpu.VMEM(sources[0].shape, sources[0].dtype)] * count,
        in_specs=[VMEM] * (1 + len(sources)),
        out_specs=[VMEM] * count,
        compiler_params=pltpu.CompilerParams(vmem_limit_bytes=12 * MIB),
        cost_estimate=pl.CostEstimate(flops=0, bytes_accessed=2 * count * size, transcendentals=0),
        name="select_panels",
    )(which, *sources)


def pack_kernel(start, size, source, *refs):
    outs, sem = refs[:-1], refs[-1]
    n = len(outs)
    copies = []
    for k, out in enumerate(outs):
        piece = lax.rem(lax.axis_index("lab") + k, n)
        row = pl.multiple_of(start + piece * size, 16)
        copies.append(pltpu.make_async_copy(source.at[pl.ds(row, size)], out, sem.at[k]))
    for copy in copies:
        copy.start()
    for copy in copies:
        copy.wait()


def pack(source, start, n):
    size = (source.shape[0] - start) // n
    shape = (size, source.shape[1])
    return pl.pallas_call(
        functools.partial(pack_kernel, start, size),
        out_shape=[pltpu.VMEM(shape, source.dtype)] * n,
        in_specs=[HBM],
        out_specs=[VMEM] * n,
        scratch_shapes=[pltpu.SemaphoreType.DMA((n,))],
        compiler_params=pltpu.CompilerParams(vmem_limit_bytes=PACK_MIB * MIB),
        name="pack_pieces",
    )(source)


def coded(high, low):
    value = (low + 128).astype(jnp.float32) * 2.0**-64
    for bit in range(7):
        value = jnp.where((high >> bit) & 1 == 1, value * 2.0 ** (1 << bit), value)
    return value


def split(value):
    high = value.astype(jnp.bfloat16)
    return high, (value - high.astype(jnp.float32)).astype(jnp.bfloat16)


def product(pair, other, dims):
    dot = functools.partial(
        lax.dot_general, dimension_numbers=(dims, ((), ())), preferred_element_type=jnp.float32
    )
    return dot(pair[1], other) + dot(pair[0], other)


def update_kernel(first, last, n, tops, size, offset, scale, *refs):
    order = circle(n)
    lab = lax.axis_index("lab")
    place = sum(jnp.where(lab == i, order.index(i), 0) for i in range(n))
    panels, refs = refs[: len(tops)], refs[len(tops) :]
    pieces, refs = refs[:n], refs[n:]
    live_ref, pick_ref, weight_ref, *refs = refs
    moment_ref = None if first else refs.pop(0)
    weight_out, moment_out, rows_ref, *refs = refs
    labels = weight_ref.shape[0]
    count = rows_ref.shape[0]
    top = 0
    for panel_ref, rows in zip(panels, tops):
        rows_ref[top : top + rows, :] = panel_ref[:rows, :]
        top += rows
    for k, piece in enumerate(pieces):
        at = lax.rem(place + n - k, n)
        plane = sum(jnp.where(at == i, order[i], 0) for i in range(n))
        row = pl.multiple_of(top + plane * size, 16)
        rows_ref[pl.ds(row, size), :] = piece[offset : offset + size, :]
    rows = rows_ref[...]
    weight = weight_ref[...]
    pair = split(weight)
    dot = functools.partial(jnp.dot, preferred_element_type=jnp.float32)
    parent = dot(pick_ref[...], pair[1]) + dot(pick_ref[...], pair[0])
    pull = pull_rate * (weight - parent)
    label = lax.broadcasted_iota(jnp.int32, (labels, LANES), 0)
    label = ((label & 127) + 128) << (label >> 7)
    label = (label.astype(jnp.float32) * live_ref[:, count:]).astype(jnp.bfloat16)
    label = jnp.concatenate([label] * (count // LANES), axis=1)
    target = jnp.zeros(label.shape, jnp.bfloat16)
    for k in range(POS):
        code = panels[0][tops[0] + k : tops[0] + k + 1, :count]
        target = jnp.where(label == code, jnp.bfloat16(1.0), target)
    scores = product(pair, rows, ((1,), (1,))) * scale
    resid = (jax.nn.sigmoid(scores) - target.astype(jnp.float32)) * live_ref[:, :count]
    resid = split(resid)
    columns = COLUMNS if last else weight.shape[1]
    copies = []
    for c in range(0, weight.shape[1], columns):
        part = slice(c, c + columns)
        grad = product(resid, rows[:, part], ((1,), (0,))) * scale + pull[:, part]
        moment = grad if first else beta_rate * moment_ref[:, part] + grad
        value = weight[:, part] - learning_rate * moment
        if not last:
            moment_out[:, part] = moment
            weight_out[:, part] = value
            continue
        weight_held, moment_held, sem = refs
        weight_held[:, part] = value
        moment_held[:, part] = moment
        for held, out in ((weight_held, weight_out), (moment_held, moment_out)):
            done = sem.at[len(copies)]
            copies.append(pltpu.make_async_copy(held.at[:, part], out.at[:, part], done))
            copies[-1].start()
    for copy in copies:
        copy.wait()


def update(panels, pieces, offset, live, pick, weight, moment, last):
    labels, width = weight.shape
    count = live.shape[1] - LANES
    tops = [panel.shape[0] for panel in panels]
    tops[0] -= POS
    size = (count - sum(tops)) // len(pieces)
    first = moment is None
    state = [weight] if first else [weight, moment]
    shape = (jax.ShapeDtypeStruct if last else pltpu.VMEM)(weight.shape, jnp.float32)
    scratch = [pltpu.VMEM((count, width), panels[0].dtype)]
    if last:
        scratch += [pltpu.VMEM(weight.shape, jnp.float32)] * 2
        scratch += [pltpu.SemaphoreType.DMA((2 * width // COLUMNS,))]
    scale = 1.0 / float(width) ** 0.5
    return pl.pallas_call(
        functools.partial(update_kernel, first, last, len(pieces), tops, size, offset, scale),
        out_shape=[shape, shape],
        in_specs=[VMEM] * (len(panels) + len(pieces) + 2 + len(state)),
        out_specs=[HBM if last else VMEM] * 2,
        scratch_shapes=scratch,
        compiler_params=pltpu.CompilerParams(vmem_limit_bytes=UPDATE_MIB * MIB),
        cost_estimate=pl.CostEstimate(
            flops=8 * labels * width * count,
            bytes_accessed=2 * count * width + 16 * labels * width,
            transcendentals=labels * count,
        ),
        name="update_block",
    )(*panels, *pieces, live, pick, *state)


def after(value, *earlier):
    return lax.optimization_barrier((value, *earlier))[0]


def send(what, value, axis, pairs, *earlier):
    value = after(value, *earlier) if earlier else value
    with jax.named_scope(what):
        return lax.ppermute(value, axis, pairs)


def local(embeddings, positives, weights, parents, owners, shortlist, counts):
    doc_index = lax.axis_index("doc")
    lab_index = lax.axis_index("lab")
    doc_count = lax.axis_size("doc")
    lab_count = lax.axis_size("lab")
    labels, width = weights.shape
    rows = embeddings.shape[0]
    home = doc_index * lab_count + lab_index
    grain = 16 * lab_count
    size = max(1, rows * LOWER // grain // 8) * 16
    top = rows - size * lab_count

    mine = pack(embeddings, top, lab_count)

    codes = coded(positives.T >> 7, positives.T & 127).astype(jnp.bfloat16)
    codes = jnp.pad(codes, ((0, 0), (0, width - rows)))
    first = top // 32 * 16
    upper = [jnp.concatenate([embeddings[:first], codes], axis=0), embeddings[first:top]]

    order = circle(lab_count)
    place_of = jnp.array([order.index(i) for i in range(lab_count)], jnp.int32)
    owner = lax.dynamic_index_in_dim(owners, doc_index, 1, keepdims=False)
    which_upper = (place_of[lab_index] - place_of[owner]) % lab_count
    which_lower = (lab_index - owner) % lab_count
    which_upper, which_lower = (
        jnp.broadcast_to(which[:, None], (STEPS, width)).astype(jnp.bfloat16)
        for which in (which_upper, which_lower)
    )
    lists = lax.dynamic_index_in_dim(shortlist, home, 1, keepdims=False)
    used = lax.dynamic_index_in_dim(counts, home, 1, keepdims=True)
    listed = lists[:, :, None] == jnp.arange(rows, dtype=jnp.int32) // TILE
    listed = listed & (jnp.arange(lists.shape[1], dtype=jnp.int32) < used)[:, :, None]
    live = jnp.any(listed, axis=1).astype(jnp.float32)
    base = (jnp.arange(STEPS, dtype=jnp.int32) * lab_count + lab_index) * labels
    unit = jnp.broadcast_to(coded(base >> 7, jnp.zeros_like(base))[:, None], (STEPS, LANES))
    live = jnp.concatenate([live, unit / 128.0], axis=1)
    parent_rows = lax.dynamic_slice_in_dim(parents, home * labels, labels, 0)
    pick = parent_rows[:, None] == jnp.arange(labels, dtype=jnp.int32)
    pick = pick.astype(jnp.bfloat16)
    prepared = (which_upper, live, pick)

    around = [(order[i], order[(i + 1) % lab_count]) for i in range(lab_count)]

    def shift(what, step, value, *earlier):
        pairs = [(i, (i - step) % doc_count) for i in range(doc_count)]
        return send(f"{what}_doc_shift_{step}", value, "doc", pairs, *earlier)

    met = [mine[0]]
    for k in range(1, lab_count):
        pairs = [(i, (i + k) % lab_count) for i in range(lab_count)]
        met.append(send(f"lower_lab_shift_{k}", mine[k], "lab", pairs))
    held = [[chunk] for chunk in upper]

    def hop(what, line, *earlier):
        line.append(send(f"{what}_lab_hop_{len(line)}", line[-1], "lab", around, *earlier))

    hop("upper_0", held[0], mine[0])
    hop("upper_1", held[1], mine[0])
    lower = select(which_lower, met)
    hop("upper_0", held[0], *prepared, lower[0])
    lower = [lower[0]] + [shift("lower", s, lower[s]) for s in range(1, STEPS)]
    parts = [[jnp.concatenate([lower[s] for s in steps], axis=0)] for steps in GROUPS]
    hop("upper_1", held[1], held[0][2])
    for r in range(3, lab_count):
        hop("upper_0", held[0], *lower[1:])
    hop("part_0", parts[0], *lower[1:])
    ahead = select(which_upper, held[0])
    panels = [[ahead[0]]] + [[shift("upper_0", s, ahead[s])] for s in range(1, STEPS)]
    for r in range(3, lab_count):
        hop("upper_1", held[1], ahead[0])
    hop("part_1", parts[1])
    found = select(which_upper, [after(held[1][0], panels[2][0]), *held[1][1:]])
    panels[0].append(found[0])
    for s in range(1, STEPS):
        panels[s].append(shift("upper_1", s, found[s], panels[s][0]))
    for r in range(2, lab_count):
        hop("part_0", parts[0], *(panels[2][:1] if r > 2 else ()))
        hop("part_1", parts[1], panels[1 if r == 2 else 2][0])

    weight, moment = weights, None
    for s in range(STEPS):
        weight, moment = update(
            panels[s],
            parts[s in GROUPS[1]],
            (s - GROUPS[s in GROUPS[1]][0]) * size,
            live[s : s + 1],
            pick,
            weight,
            moment,
            s == STEPS - 1,
        )
    return (weight, moment)


def solution(mesh):
    return jax.shard_map(
        local,
        mesh=mesh,
        in_specs=(
            P(("doc", "lab"), None),
            P(("doc", "lab"), None),
            P(("doc", "lab"), None),
            P(),
            P(),
            P(),
            P(),
        ),
        out_specs=(P(("doc", "lab"), None), P(("doc", "lab"), None)),
        check_vma=False,
    )
```

```python
import functools

import jax
import jax.numpy as jnp
from jax import lax
from jax.experimental import pallas as pl
from jax.experimental.pallas import tpu as pltpu
from jax.sharding import PartitionSpec as P

TILE = 128
STEPS = 4
POS = 16
LOWER = 4
GROUPS = ((0, 1), (2, 3))
LANES = 128
COLUMNS = 256
UPDATE_MIB = 7
PACK_MIB = 60

learning_rate = 0.1
beta_rate = 0.9
pull_rate = 1.0

VMEM = pl.BlockSpec(memory_space=pltpu.VMEM)
HBM = pl.BlockSpec(memory_space=pltpu.HBM)
MIB = 1024 * 1024


def circle(n):
    return [*range(0, 1), *range(1, n, 2), *reversed(range(2, n, 2))]


def select_kernel(n, which_ref, *refs):
    sources, outs = refs[:n], refs[n:]
    for k, out in enumerate(outs):
        which = which_ref[k : k + 1, :]
        value = sources[0][...]
        for i in range(1, n):
            value = jnp.where(which == jnp.bfloat16(i), sources[i][...], value)
        out[...] = value


def select(which, sources):
    size = sources[0].size * sources[0].dtype.itemsize
    count = which.shape[0]
    return pl.pallas_call(
        functools.partial(select_kernel, len(sources)),
        out_shape=[pltpu.VMEM(sources[0].shape, sources[0].dtype)] * count,
        in_specs=[VMEM] * (1 + len(sources)),
        out_specs=[VMEM] * count,
        compiler_params=pltpu.CompilerParams(vmem_limit_bytes=12 * MIB),
        cost_estimate=pl.CostEstimate(flops=0, bytes_accessed=2 * count * size, transcendentals=0),
        name="select_panels",
    )(which, *sources)


def pack_kernel(start, size, source, *refs):
    outs, sem = refs[:-1], refs[-1]
    n = len(outs)
    copies = []
    for k, out in enumerate(outs):
        piece = lax.rem(lax.axis_index("lab") + k, n)
        row = pl.multiple_of(start + piece * size, 16)
        copies.append(pltpu.make_async_copy(source.at[pl.ds(row, size)], out, sem.at[k]))
    for copy in copies:
        copy.start()
    for copy in copies:
        copy.wait()


def pack(source, start, n):
    size = (source.shape[0] - start) // n
    shape = (size, source.shape[1])
    return pl.pallas_call(
        functools.partial(pack_kernel, start, size),
        out_shape=[pltpu.VMEM(shape, source.dtype)] * n,
        in_specs=[HBM],
        out_specs=[VMEM] * n,
        scratch_shapes=[pltpu.SemaphoreType.DMA((n,))],
        compiler_params=pltpu.CompilerParams(vmem_limit_bytes=PACK_MIB * MIB),
        name="pack_pieces",
    )(source)


def coded(high, low):
    value = (low + 128).astype(jnp.float32) * 2.0**-64
    for bit in range(7):
        value = jnp.where((high >> bit) & 1 == 1, value * 2.0 ** (1 << bit), value)
    return value


def split(value):
    high = value.astype(jnp.bfloat16)
    return high, (value - high.astype(jnp.float32)).astype(jnp.bfloat16)


def product(pair, other, dims):
    dot = functools.partial(
        lax.dot_general, dimension_numbers=(dims, ((), ())), preferred_element_type=jnp.float32
    )
    return dot(pair[1], other) + dot(pair[0], other)


def update_kernel(first, last, n, tops, size, offset, scale, *refs):
    order = circle(n)
    lab = lax.axis_index("lab")
    place = sum(jnp.where(lab == i, order.index(i), 0) for i in range(n))
    panels, refs = refs[: len(tops)], refs[len(tops) :]
    pieces, refs = refs[:n], refs[n:]
    live_ref, pick_ref, weight_ref, *refs = refs
    moment_ref = None if first else refs.pop(0)
    weight_out, moment_out, rows_ref, *refs = refs
    labels = weight_ref.shape[0]
    count = rows_ref.shape[0]
    top = 0
    for panel_ref, rows in zip(panels, tops):
        rows_ref[top : top + rows, :] = panel_ref[:rows, :]
        top += rows
    for k, piece in enumerate(pieces):
        at = lax.rem(place + n - k, n)
        plane = sum(jnp.where(at == i, order[i], 0) for i in range(n))
        row = pl.multiple_of(top + plane * size, 16)
        rows_ref[pl.ds(row, size), :] = piece[offset : offset + size, :]
    rows = rows_ref[...]
    weight = weight_ref[...]
    pair = split(weight)
    dot = functools.partial(jnp.dot, preferred_element_type=jnp.float32)
    parent = dot(pick_ref[...], pair[1]) + dot(pick_ref[...], pair[0])
    pull = pull_rate * (weight - parent)
    label = lax.broadcasted_iota(jnp.int32, (labels, LANES), 0)
    label = ((label & 127) + 128) << (label >> 7)
    label = (label.astype(jnp.float32) * live_ref[:, count:]).astype(jnp.bfloat16)
    label = jnp.concatenate([label] * (count // LANES), axis=1)
    target = jnp.zeros(label.shape, jnp.bfloat16)
    codes = panels[0][tops[0] : tops[0] + POS, :count]
    for k in range(POS):
        target = jnp.where(label == codes[k : k + 1, :], jnp.bfloat16(1.0), target)
    scores = product(pair, rows, ((1,), (1,))) * scale
    resid = (jax.nn.sigmoid(scores) - target.astype(jnp.float32)) * live_ref[:, :count]
    resid = split(resid)
    columns = COLUMNS if last else weight.shape[1]
    copies = []
    for c in range(0, weight.shape[1], columns):
        part = slice(c, c + columns)
        grad = product(resid, rows[:, part], ((1,), (0,))) * scale + pull[:, part]
        moment = grad if first else beta_rate * moment_ref[:, part] + grad
        value = weight[:, part] - learning_rate * moment
        if not last:
            moment_out[:, part] = moment
            weight_out[:, part] = value
            continue
        weight_held, moment_held, sem = refs
        weight_held[:, part] = value
        moment_held[:, part] = moment
        for held, out in ((weight_held, weight_out), (moment_held, moment_out)):
            done = sem.at[len(copies)]
            copies.append(pltpu.make_async_copy(held.at[:, part], out.at[:, part], done))
            copies[-1].start()
    for copy in copies:
        copy.wait()


def update(panels, pieces, offset, live, pick, weight, moment, last):
    labels, width = weight.shape
    count = live.shape[1] - LANES
    tops = [panel.shape[0] for panel in panels]
    tops[0] -= POS
    size = (count - sum(tops)) // len(pieces)
    first = moment is None
    state = [weight] if first else [weight, moment]
    shape = (jax.ShapeDtypeStruct if last else pltpu.VMEM)(weight.shape, jnp.float32)
    scratch = [pltpu.VMEM((count, width), panels[0].dtype)]
    if last:
        scratch += [pltpu.VMEM(weight.shape, jnp.float32)] * 2
        scratch += [pltpu.SemaphoreType.DMA((2 * width // COLUMNS,))]
    scale = 1.0 / float(width) ** 0.5
    return pl.pallas_call(
        functools.partial(update_kernel, first, last, len(pieces), tops, size, offset, scale),
        out_shape=[shape, shape],
        in_specs=[VMEM] * (len(panels) + len(pieces) + 2 + len(state)),
        out_specs=[HBM if last else VMEM] * 2,
        scratch_shapes=scratch,
        compiler_params=pltpu.CompilerParams(vmem_limit_bytes=UPDATE_MIB * MIB),
        cost_estimate=pl.CostEstimate(
            flops=8 * labels * width * count,
            bytes_accessed=2 * count * width + 16 * labels * width,
            transcendentals=labels * count,
        ),
        name="update_block",
    )(*panels, *pieces, live, pick, *state)


def after(value, *earlier):
    return lax.optimization_barrier((value, *earlier))[0]


def send(what, value, axis, pairs, *earlier):
    value = after(value, *earlier) if earlier else value
    with jax.named_scope(what):
        return lax.ppermute(value, axis, pairs)


def local(embeddings, positives, weights, parents, owners, shortlist, counts):
    doc_index = lax.axis_index("doc")
    lab_index = lax.axis_index("lab")
    doc_count = lax.axis_size("doc")
    lab_count = lax.axis_size("lab")
    labels, width = weights.shape
    rows = embeddings.shape[0]
    home = doc_index * lab_count + lab_index
    grain = 16 * lab_count
    size = max(1, rows * LOWER // grain // 8) * 16
    top = rows - size * lab_count

    mine = pack(embeddings, top, lab_count)

    codes = coded(positives.T >> 7, positives.T & 127).astype(jnp.bfloat16)
    codes = jnp.pad(codes, ((0, 0), (0, width - rows)))
    first = top // 32 * 16
    upper = [jnp.concatenate([embeddings[:first], codes], axis=0), embeddings[first:top]]

    order = circle(lab_count)
    place_of = jnp.array([order.index(i) for i in range(lab_count)], jnp.int32)
    owner = lax.dynamic_index_in_dim(owners, doc_index, 1, keepdims=False)
    which_upper = (place_of[lab_index] - place_of[owner]) % lab_count
    which_lower = (lab_index - owner) % lab_count
    which_upper, which_lower = (
        jnp.broadcast_to(which[:, None], (STEPS, width)).astype(jnp.bfloat16)
        for which in (which_upper, which_lower)
    )
    lists = lax.dynamic_index_in_dim(shortlist, home, 1, keepdims=False)
    used = lax.dynamic_index_in_dim(counts, home, 1, keepdims=True)
    listed = lists[:, :, None] == jnp.arange(rows, dtype=jnp.int32) // TILE
    listed = listed & (jnp.arange(lists.shape[1], dtype=jnp.int32) < used)[:, :, None]
    live = jnp.any(listed, axis=1).astype(jnp.float32)
    base = (jnp.arange(STEPS, dtype=jnp.int32) * lab_count + lab_index) * labels
    unit = jnp.broadcast_to(coded(base >> 7, jnp.zeros_like(base))[:, None], (STEPS, LANES))
    live = jnp.concatenate([live, unit / 128.0], axis=1)
    parent_rows = lax.dynamic_slice_in_dim(parents, home * labels, labels, 0)
    pick = parent_rows[:, None] == jnp.arange(labels, dtype=jnp.int32)
    pick = pick.astype(jnp.bfloat16)
    prepared = (which_upper, live, pick)

    around = [(order[i], order[(i + 1) % lab_count]) for i in range(lab_count)]

    def shift(what, step, value, *earlier):
        pairs = [(i, (i - step) % doc_count) for i in range(doc_count)]
        return send(f"{what}_doc_shift_{step}", value, "doc", pairs, *earlier)

    met = [mine[0]]
    for k in range(1, lab_count):
        pairs = [(i, (i + k) % lab_count) for i in range(lab_count)]
        met.append(send(f"lower_lab_shift_{k}", mine[k], "lab", pairs))
    held = [[chunk] for chunk in upper]

    def hop(what, line, *earlier):
        line.append(send(f"{what}_lab_hop_{len(line)}", line[-1], "lab", around, *earlier))

    hop("upper_0", held[0], mine[0])
    hop("upper_1", held[1], mine[0])
    lower = select(which_lower, met)
    hop("upper_0", held[0], *prepared, lower[0])
    lower = [lower[0]] + [shift("lower", s, lower[s]) for s in range(1, STEPS)]
    parts = [[jnp.concatenate([lower[s] for s in steps], axis=0)] for steps in GROUPS]
    hop("upper_1", held[1], held[0][2])
    for r in range(3, lab_count):
        hop("upper_0", held[0], *lower[1:])
    hop("part_0", parts[0], *lower[1:])
    ahead = select(which_upper, held[0])
    panels = [[ahead[0]]] + [[shift("upper_0", s, ahead[s])] for s in range(1, STEPS)]
    for r in range(3, lab_count):
        hop("upper_1", held[1], ahead[0])
    hop("part_1", parts[1])
    found = select(which_upper, [after(held[1][0], panels[2][0]), *held[1][1:]])
    panels[0].append(found[0])
    for s in range(1, STEPS):
        panels[s].append(shift("upper_1", s, found[s], panels[s][0]))
    for r in range(2, lab_count):
        hop("part_0", parts[0], *(panels[2][:1] if r > 2 else ()))
        hop("part_1", parts[1], panels[1 if r == 2 else 2][0])

    weight, moment = weights, None
    for s in range(STEPS):
        weight, moment = update(
            panels[s],
            parts[s in GROUPS[1]],
            (s - GROUPS[s in GROUPS[1]][0]) * size,
            live[s : s + 1],
            pick,
            weight,
            moment,
            s == STEPS - 1,
        )
    return (weight, moment)


def solution(mesh):
    return jax.shard_map(
        local,
        mesh=mesh,
        in_specs=(
            P(("doc", "lab"), None),
            P(("doc", "lab"), None),
            P(("doc", "lab"), None),
            P(),
            P(),
            P(),
            P(),
        ),
        out_specs=(P(("doc", "lab"), None), P(("doc", "lab"), None)),
        check_vma=False,
    )
```

```python
import functools

import jax
import jax.numpy as jnp
from jax import lax
from jax.experimental import pallas as pl
from jax.experimental.pallas import tpu as pltpu
from jax.sharding import PartitionSpec as P

TILE = 128
STEPS = 4
POS = 16
LOWER = 4
GROUPS = ((0, 1), (2, 3))
LANES = 128
COLUMNS = 256
UPDATE_MIB = 7
PACK_MIB = 60

learning_rate = 0.1
beta_rate = 0.9
pull_rate = 1.0

VMEM = pl.BlockSpec(memory_space=pltpu.VMEM)
HBM = pl.BlockSpec(memory_space=pltpu.HBM)
MIB = 1024 * 1024


def circle(n):
    return [*range(0, 1), *range(1, n, 2), *reversed(range(2, n, 2))]


def select_kernel(n, which_ref, *refs):
    sources, outs = refs[:n], refs[n:]
    for k, out in enumerate(outs):
        which = which_ref[k : k + 1, :]
        value = sources[0][...]
        for i in range(1, n):
            value = jnp.where(which == jnp.bfloat16(i), sources[i][...], value)
        out[...] = value


def select(which, sources):
    size = sources[0].size * sources[0].dtype.itemsize
    count = which.shape[0]
    return pl.pallas_call(
        functools.partial(select_kernel, len(sources)),
        out_shape=[pltpu.VMEM(sources[0].shape, sources[0].dtype)] * count,
        in_specs=[VMEM] * (1 + len(sources)),
        out_specs=[VMEM] * count,
        compiler_params=pltpu.CompilerParams(vmem_limit_bytes=12 * MIB),
        cost_estimate=pl.CostEstimate(flops=0, bytes_accessed=2 * count * size, transcendentals=0),
        name="select_panels",
    )(which, *sources)


def pack_kernel(start, size, source, *refs):
    outs, sem = refs[:-1], refs[-1]
    n = len(outs)
    copies = []
    for k, out in enumerate(outs):
        piece = lax.rem(lax.axis_index("lab") + k, n)
        row = pl.multiple_of(start + piece * size, 16)
        copies.append(pltpu.make_async_copy(source.at[pl.ds(row, size)], out, sem.at[k]))
    for copy in copies:
        copy.start()
    for copy in copies:
        copy.wait()


def pack(source, start, n):
    size = (source.shape[0] - start) // n
    shape = (size, source.shape[1])
    return pl.pallas_call(
        functools.partial(pack_kernel, start, size),
        out_shape=[pltpu.VMEM(shape, source.dtype)] * n,
        in_specs=[HBM],
        out_specs=[VMEM] * n,
        scratch_shapes=[pltpu.SemaphoreType.DMA((n,))],
        compiler_params=pltpu.CompilerParams(vmem_limit_bytes=PACK_MIB * MIB),
        name="pack_pieces",
    )(source)


def coded(high, low):
    value = (low + 128).astype(jnp.float32) * 2.0**-64
    for bit in range(7):
        value = jnp.where((high >> bit) & 1 == 1, value * 2.0 ** (1 << bit), value)
    return value


def split(value):
    high = value.astype(jnp.bfloat16)
    return high, (value - high.astype(jnp.float32)).astype(jnp.bfloat16)


def product(pair, other, dims):
    dot = functools.partial(
        lax.dot_general, dimension_numbers=(dims, ((), ())), preferred_element_type=jnp.float32
    )
    return dot(pair[1], other) + dot(pair[0], other)


def update_kernel(first, last, n, tops, size, offset, scale, *refs):
    order = circle(n)
    lab = lax.axis_index("lab")
    place = sum(jnp.where(lab == i, order.index(i), 0) for i in range(n))
    panels, refs = refs[: len(tops)], refs[len(tops) :]
    pieces, refs = refs[:n], refs[n:]
    live_ref, pick_ref, weight_ref, *refs = refs
    moment_ref = None if first else refs.pop(0)
    weight_out, moment_out, rows_ref, *refs = refs
    labels = weight_ref.shape[0]
    count = rows_ref.shape[0]
    top = 0
    for panel_ref, rows in zip(panels, tops):
        rows_ref[top : top + rows, :] = panel_ref[:rows, :]
        top += rows
    for k, piece in enumerate(pieces):
        at = lax.rem(place + n - k, n)
        plane = sum(jnp.where(at == i, order[i], 0) for i in range(n))
        row = pl.multiple_of(top + plane * size, 16)
        rows_ref[pl.ds(row, size), :] = piece[offset : offset + size, :]
    rows = rows_ref[...]
    weight = weight_ref[...]
    pair = split(weight)
    dot = functools.partial(jnp.dot, preferred_element_type=jnp.float32)
    parent = dot(pick_ref[...], pair[1]) + dot(pick_ref[...], pair[0])
    pull = pull_rate * (weight - parent)
    label = lax.broadcasted_iota(jnp.int32, (labels, LANES), 0)
    label = ((label & 127) + 128) << (label >> 7)
    label = (label.astype(jnp.float32) * live_ref[:, count:]).astype(jnp.bfloat16)
    label = jnp.concatenate([label] * (count // LANES), axis=1)
    target = jnp.zeros(label.shape, jnp.bfloat16)
    codes = panels[0][tops[0] : tops[0] + POS, :count]
    for k in range(POS):
        target = jnp.where(label == codes[k : k + 1, :], jnp.bfloat16(1.0), target)
    scores = product(pair, rows, ((1,), (1,))) * scale
    resid = (jax.nn.sigmoid(scores) - target.astype(jnp.float32)) * live_ref[:, :count]
    resid = split(resid)
    columns = COLUMNS if last else weight.shape[1]
    copies = []
    for c in range(0, weight.shape[1], columns):
        part = slice(c, c + columns)
        grad = product(resid, rows[:, part], ((1,), (0,))) * scale + pull[:, part]
        moment = grad if first else beta_rate * moment_ref[:, part] + grad
        value = weight[:, part] - learning_rate * moment
        if not last:
            moment_out[:, part] = moment
            weight_out[:, part] = value
            continue
        weight_held, moment_held, sem = refs
        weight_held[:, part] = value
        moment_held[:, part] = moment
        for held, out in ((weight_held, weight_out), (moment_held, moment_out)):
            done = sem.at[len(copies)]
            copies.append(pltpu.make_async_copy(held.at[:, part], out.at[:, part], done))
            copies[-1].start()
    for copy in copies:
        copy.wait()


def update(panels, pieces, offset, live, pick, weight, moment, last):
    labels, width = weight.shape
    count = live.shape[1] - LANES
    tops = [panel.shape[0] for panel in panels]
    tops[0] -= POS
    size = (count - sum(tops)) // len(pieces)
    first = moment is None
    state = [weight] if first else [weight, moment]
    shape = (jax.ShapeDtypeStruct if last else pltpu.VMEM)(weight.shape, jnp.float32)
    scratch = [pltpu.VMEM((count, width), panels[0].dtype)]
    if last:
        scratch += [pltpu.VMEM(weight.shape, jnp.float32)] * 2
        scratch += [pltpu.SemaphoreType.DMA((2 * width // COLUMNS,))]
    scale = 1.0 / float(width) ** 0.5
    return pl.pallas_call(
        functools.partial(update_kernel, first, last, len(pieces), tops, size, offset, scale),
        out_shape=[shape, shape],
        in_specs=[VMEM] * (len(panels) + len(pieces) + 2 + len(state)),
        out_specs=[HBM if last else VMEM] * 2,
        scratch_shapes=scratch,
        compiler_params=pltpu.CompilerParams(vmem_limit_bytes=UPDATE_MIB * MIB),
        cost_estimate=pl.CostEstimate(
            flops=8 * labels * width * count,
            bytes_accessed=2 * count * width + 16 * labels * width,
            transcendentals=labels * count,
        ),
        name="update_block",
    )(*panels, *pieces, live, pick, *state)


def after(value, *earlier):
    return lax.optimization_barrier((value, *earlier))[0]


def send(what, value, axis, pairs, *earlier):
    value = after(value, *earlier) if earlier else value
    with jax.named_scope(what):
        return lax.ppermute(value, axis, pairs)


def local(embeddings, positives, weights, parents, owners, shortlist, counts):
    doc_index = lax.axis_index("doc")
    lab_index = lax.axis_index("lab")
    doc_count = lax.axis_size("doc")
    lab_count = lax.axis_size("lab")
    labels, width = weights.shape
    rows = embeddings.shape[0]
    home = doc_index * lab_count + lab_index
    grain = 16 * lab_count
    size = max(1, rows * LOWER // grain // 8) * 16
    top = rows - size * lab_count

    mine = pack(embeddings, top, lab_count)

    codes = coded(positives.T >> 7, positives.T & 127).astype(jnp.bfloat16)
    codes = jnp.pad(codes, ((0, 0), (0, width - rows)))
    first = top // 32 * 16
    upper = [jnp.concatenate([embeddings[:first], codes], axis=0), embeddings[first:top]]

    order = circle(lab_count)
    place_of = jnp.array([order.index(i) for i in range(lab_count)], jnp.int32)
    owner = lax.dynamic_index_in_dim(owners, doc_index, 1, keepdims=False)
    which_upper = (place_of[lab_index] - place_of[owner]) % lab_count
    which_lower = (lab_index - owner) % lab_count
    which_upper, which_lower = (
        jnp.broadcast_to(which[:, None], (STEPS, width)).astype(jnp.bfloat16)
        for which in (which_upper, which_lower)
    )
    lists = lax.dynamic_index_in_dim(shortlist, home, 1, keepdims=False)
    used = lax.dynamic_index_in_dim(counts, home, 1, keepdims=True)
    listed = lists[:, :, None] == jnp.arange(rows, dtype=jnp.int32) // TILE
    listed = listed & (jnp.arange(lists.shape[1], dtype=jnp.int32) < used)[:, :, None]
    live = jnp.any(listed, axis=1).astype(jnp.float32)
    base = (jnp.arange(STEPS, dtype=jnp.int32) * lab_count + lab_index) * labels
    unit = jnp.broadcast_to(coded(base >> 7, jnp.zeros_like(base))[:, None], (STEPS, LANES))
    live = jnp.concatenate([live, unit / 128.0], axis=1)
    parent_rows = lax.dynamic_slice_in_dim(parents, home * labels, labels, 0)
    pick = parent_rows[:, None] == jnp.arange(labels, dtype=jnp.int32)
    pick = pick.astype(jnp.bfloat16)
    prepared = (which_upper, live, pick)

    around = [(order[i], order[(i + 1) % lab_count]) for i in range(lab_count)]

    def shift(what, step, value, *earlier):
        pairs = [(i, (i - step) % doc_count) for i in range(doc_count)]
        return send(f"{what}_doc_shift_{step}", value, "doc", pairs, *earlier)

    met = [mine[0]]
    for k in range(1, lab_count):
        pairs = [(i, (i + k) % lab_count) for i in range(lab_count)]
        met.append(send(f"lower_lab_shift_{k}", mine[k], "lab", pairs))
    held = [[chunk] for chunk in upper]

    def hop(what, line, *earlier):
        line.append(send(f"{what}_lab_hop_{len(line)}", line[-1], "lab", around, *earlier))

    hop("upper_0", held[0], mine[0])
    hop("upper_1", held[1], mine[0])
    lower = select(which_lower, met)
    hop("upper_0", held[0], *prepared, lower[0])
    lower = [lower[0]] + [shift("lower", s, lower[s]) for s in range(1, STEPS)]
    parts = [[jnp.concatenate([lower[s] for s in steps], axis=0)] for steps in GROUPS]
    hop("upper_1", held[1], held[0][2])
    for r in range(3, lab_count):
        hop("upper_0", held[0], *lower[1:])
    hop("part_0", parts[0], *lower[1:])
    ahead = select(which_upper, held[0])
    panels = [[ahead[0]]] + [[shift("upper_0", s, ahead[s])] for s in range(1, STEPS)]
    for r in range(3, lab_count):
        hop("upper_1", held[1], panels[1][0])
    hop("part_1", parts[1])
    found = select(which_upper, [after(held[1][0], panels[2][0]), *held[1][1:]])
    panels[0].append(found[0])
    for s in range(1, STEPS):
        panels[s].append(shift("upper_1", s, found[s], panels[s][0]))
    for r in range(2, lab_count):
        hop("part_0", parts[0], *(panels[2][:1] if r > 2 else ()))
        hop("part_1", parts[1], panels[1 if r == 2 else 2][0])

    weight, moment = weights, None
    for s in range(STEPS):
        weight, moment = update(
            panels[s],
            parts[s in GROUPS[1]],
            (s - GROUPS[s in GROUPS[1]][0]) * size,
            live[s : s + 1],
            pick,
            weight,
            moment,
            s == STEPS - 1,
        )
    return (weight, moment)


def solution(mesh):
    return jax.shard_map(
        local,
        mesh=mesh,
        in_specs=(
            P(("doc", "lab"), None),
            P(("doc", "lab"), None),
            P(("doc", "lab"), None),
            P(),
            P(),
            P(),
            P(),
        ),
        out_specs=(P(("doc", "lab"), None), P(("doc", "lab"), None)),
        check_vma=False,
    )
```
